32 devices in a mesh: grp: 2 (over y), gx: 4 (over z), gy: 4 (over x, core).
Axes of the slice: x: 2, y: 2, z: 4, core: 2. Of those that a mesh axis runs over, the one named last changes fastest.
Arguments:
- counts: int32 [256, 256, 256], P(('grp', 'gx'), 'gy'), parts along dimension 0, may hold values from -40 to 999
Outputs:
- denoised: float32 [256, 256, 256], P(('grp', 'gx'), 'gy'), parts along dimension 0
The draws below stay inside these ranges and needn't reach their ends.
There are 2 independent parts, one for each index of `grp`. The reference program is written for one: setup_inputs(seed, part) draws one part's arguments, and reference() takes and returns one part's arrays. A program takes and returns all parts, laid end to end along the dimension named above; each array names one. Nothing has to cross between parts.
All inputs are finite; a program needn't handle non-finite values.
Results may differ from the reference program's by a relative error of at most 0.00005.
Values sent between devices are 32-bit elements; how exact they have to be, the bound alone decides.
A program may use at most 64 MiB of HBM per device.

```python
import math
import jax
import jax.numpy as jnp
from jax import lax

NT = 256
LEVELS = 3
ITERS = 2
NX = 128
NY = 256


def plant(entries, own_key, low, top_value):
    place = [jax.random.randint(jax.random.fold_in(own_key, axis), (), 0, length) for axis, length in enumerate(entries.shape)]
    longest = entries.shape.index(max(entries.shape))
    beside = place[:longest] + [(place[longest] + 1) % entries.shape[longest]] + place[longest + 1:]
    return entries.at[tuple(place)].set(low).at[tuple(beside)].set(top_value)


def setup_inputs(seed: int = 0, part: int = 0) -> dict:
    keys = jax.random.split(jax.random.key(seed), 2)
    own_keys = jax.random.split(jax.random.fold_in(keys[1], part), 2)
    counts = plant(jax.random.randint(own_keys[0], (NX, NY, NT), -40, 1000), jax.random.fold_in(own_keys[0], 1), -40, 999).astype(jnp.int32)
    return {"counts": counts}


ROOT_THREE = math.sqrt(3.0)
TAP_SCALE = 4.0 * math.sqrt(2.0)
LOW_TAPS = [(1.0 + ROOT_THREE) / TAP_SCALE, (3.0 + ROOT_THREE) / TAP_SCALE, (3.0 - ROOT_THREE) / TAP_SCALE, (1.0 - ROOT_THREE) / TAP_SCALE]
HIGH_TAPS = [LOW_TAPS[3], -LOW_TAPS[2], LOW_TAPS[1], -LOW_TAPS[0]]
STEP_SIZE = 1.0
THRESHOLD = 0.1

def analyse(values, axis_dim):
    length = values.shape[axis_dim]
    low_part = None
    high_part = None
    for tap_index in range(4):
        rolled = jnp.roll(values, -tap_index, axis=axis_dim)
        picked = lax.slice_in_dim(rolled, 0, length, 2, axis_dim)
        if low_part is None:
            low_part = LOW_TAPS[tap_index] * picked
            high_part = HIGH_TAPS[tap_index] * picked
        else:
            low_part = low_part + LOW_TAPS[tap_index] * picked
            high_part = high_part + HIGH_TAPS[tap_index] * picked
    return (low_part, high_part)

def synthesise(low_part, high_part, axis_dim):
    summed = None
    for tap_index in range(4):
        weighted = LOW_TAPS[tap_index] * low_part + HIGH_TAPS[tap_index] * high_part
        spread = jnp.stack([weighted, jnp.zeros_like(weighted)], axis=axis_dim + 1)
        new_shape = list(weighted.shape)
        new_shape[axis_dim] = new_shape[axis_dim] * 2
        spread = spread.reshape(new_shape)
        rolled = jnp.roll(spread, tap_index, axis=axis_dim)
        summed = rolled if summed is None else summed + rolled
    return summed

def forward_all(volume):
    details = []
    approx = volume
    for level_no in range(LEVELS):
        subbands = []
        for x_band in analyse(approx, 0):
            for y_band in analyse(x_band, 1):
                t_low, t_high = analyse(y_band, 2)
                subbands.append(t_low)
                subbands.append(t_high)
        approx = subbands[0]
        details.append(subbands[1:])
    return (details, approx)

def inverse_all(details, approx):
    current = approx
    for level_no in reversed(range(LEVELS)):
        subbands = [current] + list(details[level_no])
        x_parts = []
        for x_pick in range(2):
            y_parts = []
            for y_pick in range(2):
                first = subbands[4 * x_pick + 2 * y_pick]
                second = subbands[4 * x_pick + 2 * y_pick + 1]
                y_parts.append(synthesise(first, second, 2))
            x_parts.append(synthesise(y_parts[0], y_parts[1], 1))
        current = synthesise(x_parts[0], x_parts[1], 0)
    return current

def shrink(values):
    return values - jnp.clip(values, -THRESHOLD, THRESHOLD)

def reference(counts):
    scaled = counts.astype(jnp.float32)
    observed = scaled * (1.0 / 64.0)
    weight = 1.0 / (1.0 + jnp.abs(scaled) * (1.0 / 64.0))
    grad_details, grad_approx = forward_all(-(weight * observed))
    details = [[shrink(-STEP_SIZE * entry) for entry in level_bands] for level_bands in grad_details]
    approx = -STEP_SIZE * grad_approx
    for turn_no in range(ITERS - 1):
        rebuilt = inverse_all(details, approx)
        grad_details, grad_approx = forward_all(weight * (rebuilt - observed))
        details = [[shrink(old_entry - STEP_SIZE * new_entry) for old_entry, new_entry in zip(old_bands, new_bands)] for old_bands, new_bands in zip(details, grad_details)]
        approx = approx - STEP_SIZE * grad_approx
    return inverse_all(details, approx)
```

```python
import functools
import math

import jax
import jax.numpy as jnp
from jax import lax
from jax.experimental import pallas as pl
from jax.experimental.pallas import tpu as pltpu
from jax.sharding import PartitionSpec as P

ROOT_THREE = math.sqrt(3.0)
TAP_SCALE = 4.0 * math.sqrt(2.0)
H = [
    (1.0 + ROOT_THREE) / TAP_SCALE,
    (3.0 + ROOT_THREE) / TAP_SCALE,
    (3.0 - ROOT_THREE) / TAP_SCALE,
    (1.0 - ROOT_THREE) / TAP_SCALE,
]
G = [H[3], -H[2], H[1], -H[0]]
RATIO = 2.0 - ROOT_THREE
SPATIAL_SCALE = H[0] * H[0]
THRESHOLD = 0.1
MESH = pl.DeviceIdType.MESH
F32 = jnp.float32
BF16 = jnp.bfloat16

PLACES = [36, 39, 0, 2, 3, 38]


def shrink(values):
    return values - jnp.clip(values, -THRESHOLD, THRESHOLD)


def p_of(even, odd):
    return even + ROOT_THREE * odd


def q_of(even, odd):
    return ROOT_THREE * even - odd


def q_even(even, odd):
    return even - (1.0 / ROOT_THREE) * odd


def low_of(p, q_after):
    return p + RATIO * q_after


def high_of(p, q_after):
    return q_after - RATIO * p


def loop(count, body, unroll=4):
    def step(i, carry):
        body(i)
        return carry

    lax.fori_loop(0, count, step, 0, unroll=unroll)


def rows(start, size):
    return pl.ds(pl.multiple_of(start, 8), size)


def build_matrix(ref, length, padded, transposed):
    t = lax.broadcasted_iota(jnp.int32, (padded, padded), 1 if transposed else 0)
    c = lax.broadcasted_iota(jnp.int32, (padded, padded), 0 if transposed else 1)
    half = c >= length // 2
    j = (t - 2 * jnp.where(half, c - length // 2, c)) & (length - 1)
    value = jnp.zeros((padded, padded), F32)
    for tap in range(4):
        tap_value = jnp.where(half, G[tap] * SPATIAL_SCALE, H[tap] * SPATIAL_SCALE)
        value = jnp.where(j == tap, tap_value, value)
    if padded > length:
        value = jnp.where((t < length) & (c < length), value, 0.0)
    high = value.astype(BF16)
    low = (value - high.astype(F32)).astype(BF16)
    ref[0:padded, :] = high
    ref[padded : 2 * padded, :] = high
    ref[2 * padded : 3 * padded, :] = low


def times(values, matrix_ref):
    high = values.astype(BF16)
    low = (values - high.astype(F32)).astype(BF16)
    left = jnp.concatenate([high, low, high], axis=1)
    return jnp.dot(left, matrix_ref[...], preferred_element_type=F32)


def functionals(entry, count, q_last):
    def low2(i):
        return low_of(p_of(entry(i), entry(i + 1)), q_of(entry(i + 2), entry(i + 3)))

    n = count - 8
    return [
        q_last(entry(0), entry(1)),
        q_last(low2(0), low2(2)),
        p_of(entry(n + 4), entry(n + 5)),
        entry(n + 6),
        entry(n + 7),
        p_of(low2(n), low2(n + 2)),
    ]


def kernel(
    nx, ny,
    counts_hbm, out, counts, m1, m1t, m2, m2t, m3, m3t,
    t0, c1, e1, t2, a2, c2, e2, t3, a3, c3,
    s3, p3, d2, s2, p2, d1, s1, reb, halo,
    f0x, f0y, f0c, f0yr, f0cr,
    f1x, f1y, f1xr, f1yr,
    i1x, i1y, i1c, i1xr, i1yr, i1cr,
    local_sem, send_sem, recv_sem,
):
    gx = lax.axis_index("gx")
    gy = lax.axis_index("gy")

    def device(dx, dy):
        where = {}
        if dx:
            where["gx"] = lax.rem(gx + dx + nx, nx)
        if dy:
            where["gy"] = lax.rem(gy + dy + ny, ny)
        return where

    load = pltpu.make_async_copy(counts_hbm, counts, local_sem.at[0])
    load.start()

    barrier = pltpu.get_barrier_semaphore()
    around = [(dx, dy) for dx in (-1, 0, 1) for dy in (-1, 0, 1) if dx or dy]
    for dx, dy in around:
        pl.semaphore_signal(barrier, inc=1, device_id=device(dx, dy), device_id_type=MESH)

    def send(first_sem, transfers):
        copies = []
        for n, (source, target, dx, dy) in enumerate(transfers):
            copy = pltpu.make_async_remote_copy(
                src_ref=source,
                dst_ref=target,
                send_sem=send_sem.at[first_sem + n],
                recv_sem=recv_sem.at[first_sem + n],
                device_id=device(dx, dy),
                device_id_type=MESH,
            )
            copy.start()
            copies.append(copy)
        return copies

    def wait(copies):
        for copy in copies:
            copy.wait()

    build_matrix(m1, 256, 256, False)
    build_matrix(m1t, 256, 256, True)
    build_matrix(m2, 128, 128, False)
    build_matrix(m2t, 128, 128, True)
    build_matrix(m3, 64, 128, False)
    build_matrix(m3t, 64, 128, True)
    for tb in range(2):
        t0[tb, pl.ds(65, 33, stride=72), :] = jnp.zeros((33, 128), F32)
    for place in (1, 37):
        e1[pl.ds(place, 22, stride=40), :] = jnp.zeros((22, 128), F32)
    for place in (1, 21):
        e2[pl.ds(place, 12, stride=24), :] = jnp.zeros((12, 128), F32)
    for b in range(7):
        c1[b, 0:40, :] = jnp.zeros((40, 128), F32)
        c1[b, pl.ds(47, 16, stride=40), :] = jnp.zeros((16, 128), F32)
    for th in range(2):
        for b in range(1, 4):
            s1[th, b, 0:40, :] = jnp.zeros((40, 128), F32)
    f0c[...] = jnp.zeros((8, 128), F32)
    i1c[...] = jnp.zeros((8, 128), F32)
    f1y[...] = jnp.zeros((6, 32, 128), F32)
    load.wait()

    def residual(count, rebuilt):
        observed = count.astype(F32) * (1.0 / 64.0)
        weight = 1.0 / (1.0 + jnp.abs(observed))
        if rebuilt is None:
            return weight * observed
        return weight * (observed - rebuilt)

    def iteration(number):
        first = number == 0
        sem = 14 * number

        def old(ref, *index):
            return 0.0 if first else ref[index]

        def time_rows(n):
            count = counts[pl.ds(n * 4, 4)].reshape(256, 256)
            if first:
                values = residual(count, None)
            else:
                rebuilt = jnp.concatenate(
                    [reb[0, rows(n * 256, 256), :], reb[1, rows(n * 256, 256), :]], axis=1
                )
                values = residual(count, rebuilt)
            result = times(values, m1)
            for i in range(4):
                for tb in range(2):
                    t0[tb, rows((n * 4 + i) * 72, 64), :] = result[
                        i * 64 : (i + 1) * 64, tb * 128 : (tb + 1) * 128
                    ]

        loop(8, time_rows)

        for tb in range(2):
            f0x[tb] = q_of(t0[tb, 0:64, :], t0[tb, 72:136, :])
            f0y[tb] = q_even(t0[tb, pl.ds(0, 32, stride=72), :], t0[tb, pl.ds(1, 32, stride=72), :])
            f0c[tb : tb + 1, :] = q_even(f0x[tb, 0:1, :], f0x[tb, 1:2, :])
        if first:
            pl.semaphore_wait(barrier, 8)
        f0 = send(sem, [
            (f0x, t0.at[:, 2304:2368, :], -1, 0),
            (f0y, f0yr, 0, -1),
            (f0c, f0cr, -1, -1),
        ])

        def y_level1(row, chunk, tb):
            e = [t0[tb, pl.ds(row * 72 + 16 * chunk + j, 8, stride=2), :] for j in range(4)]
            p, q = p_of(e[0], e[1]), q_of(e[2], e[3])
            return [low_of(p, q), high_of(p, q)]

        def level1_store(k, chunk, tb, yb, p, q):
            for xb in range(2):
                value = high_of(p, q) if xb else low_of(p, q)
                band = 4 * xb + 2 * yb + tb
                if band == 0:
                    e1[pl.ds((k + 4) * 40 + 4 + 8 * chunk, 8), :] = value
                else:
                    place = rows((k + 1) * 40 + 8 + 8 * chunk, 8)
                    c1[band - 1, place, :] = shrink(old(c1, band - 1, place, slice(None)) + value)

        def level1(chunks):
            parts = [(chunk, tb) for chunk in chunks for tb in range(2)]

            def pair(k):
                result = []
                for chunk, tb in parts:
                    first_row = y_level1(2 * k, chunk, tb)
                    second_row = y_level1(2 * k + 1, chunk, tb)
                    for yb in range(2):
                        result.append((first_row[yb], second_row[yb]))
                return result

            def step(i, ps):
                k = i + 1
                after = pair(k)
                n = 0
                for chunk, tb in parts:
                    for yb in range(2):
                        level1_store(i, chunk, tb, yb, ps[n], q_of(*after[n]))
                        n += 1
                return tuple(p_of(*one) for one in after)

            return lax.fori_loop(0, 15, step, tuple(p_of(*one) for one in pair(0)), unroll=3)

        def level1_last(chunks, ps):
            n = 0
            for chunk in chunks:
                for tb in range(2):
                    halo_row = y_level1(32, chunk, tb)
                    for yb in range(2):
                        level1_store(15, chunk, tb, yb, ps[n], halo_row[yb])
                        n += 1

        inner = level1((0, 1, 2))
        wait(f0)
        for tb in range(2):
            t0[tb, pl.ds(64, 32, stride=72), :] = f0yr[tb]
            t0[tb, 2368:2369, :] = f0cr[tb : tb + 1, :]
        level1_last((0, 1, 2), inner)
        level1_last((3,), level1((3,)))

        for n, value in enumerate(
            functionals(lambda i: e1[(4 + i) * 40 + 4 : (4 + i) * 40 + 36, :], 16, q_of)
        ):
            f1x[n * 32 : (n + 1) * 32, :] = value
        for start, size, stride, target, offset in ((164, 16, 40, 0, e1), (0, 2, 32, 16, f1x), (64, 4, 32, 24, f1x)):
            for n, value in enumerate(
                functionals(lambda i: offset[pl.ds(start + i, size, stride=stride), :], 32, q_even)
            ):
                f1y[n, target : target + size, :] = value
        xr, yr = f1xr.at[number], f1yr.at[number]
        f1 = send(sem + 3, [
            (f1x.at[0:64], xr.at[0:64], -1, 0),
            (f1x.at[64:192], xr.at[64:192], 1, 0),
            (f1y.at[0:2, 0:16], yr.at[0:2, 0:16], 0, -1),
            (f1y.at[2:6, 0:16], yr.at[2:6, 0:16], 0, 1),
            (f1y.at[0:2, 16:24], yr.at[0:2, 16:24], -1, -1),
            (f1y.at[2:6, 16:24], yr.at[2:6, 16:24], -1, 1),
            (f1y.at[0:2, 24:32], yr.at[0:2, 24:32], 1, -1),
            (f1y.at[2:6, 24:32], yr.at[2:6, 24:32], 1, 1),
        ])

        def i1_rows(read):
            bands = [read(b) for b in range(7)]
            return bands, [bands[3], bands[4] + RATIO * bands[0], bands[5] + RATIO * bands[1], bands[6] + RATIO * bands[2]]

        _, values = i1_rows(lambda b: c1[b, 648:680, :])
        for n in range(4):
            i1x[n * 32 : (n + 1) * 32, :] = values[n]
        bands, _ = i1_rows(lambda b: c1[b, pl.ds(79, 16, stride=40), :])
        values = [bands[1], bands[2] + RATIO * bands[0], bands[5] + RATIO * bands[3], bands[6] + RATIO * bands[4]]
        for n in range(4):
            i1y[n * 16 : (n + 1) * 16, :] = values[n]
        _, values = i1_rows(lambda b: c1[b, 679:680, :])
        for n in range(2):
            i1c[n : n + 1, :] = RATIO * values[n] + values[2 + n]
        i1 = send(sem + 11, [(i1x, i1xr, 1, 0), (i1y, i1yr, 0, 1), (i1c, i1cr, 1, 1)])

        def time_up1_own(n):
            place = rows(40 + n * 128, 128)
            for b in range(1, 4):
                values = jnp.concatenate([c1[2 * b - 1, place, :], c1[2 * b, place, :]], axis=1)
                result = times(values, m1t)
                s1[0, b, place, :] = result[:, :128]
                s1[1, b, place, :] = result[:, 128:]

        loop(5, time_up1_own, unroll=5)
        wait(f1)
        e1[804:836, :] = xr[0:32, :]
        e1[844:876, :] = xr[32:64, :]
        for n in range(4):
            e1[n * 40 + 4 : n * 40 + 36, :] = xr[64 + n * 32 : 96 + n * 32, :]
        for n, place in enumerate(PLACES):
            e1[pl.ds(160 + place, 16, stride=40), :] = yr[n, 0:16, :]
            e1[pl.ds(800 + place, 2, stride=40), :] = yr[n, 16:18, :]
            e1[pl.ds(place, 4, stride=40), :] = yr[n, 24:28, :]

        def time_level2(n):
            t2[rows(n * 176, 176), :] = times(e1[rows(n * 176, 176), :], m2)

        loop(5, time_level2, unroll=5)

        def pairs(row, before, first_pair, count, last):
            ps = [row(before), p_of(row(first_pair), row(first_pair + 1))]
            qs = [q_of(row(first_pair), row(first_pair + 1))]
            return ps, qs

        def t2_row(i):
            return t2[i * 40 : (i + 1) * 40, :]

        p_now, q_after = t2_row(0), None
        for k in range(-2, 8):
            if k == 7:
                q_after, p_after = t2_row(20), None
            else:
                m = 1 if k == -2 else 6 + 2 * k
                even, odd = t2_row(m), t2_row(m + 1)
                q_after, p_after = q_of(even, odd), p_of(even, odd)
            n = (k + 2) * 40
            a2[0, n : n + 40, :] = low_of(p_now, q_after)
            a2[1, n : n + 40, :] = high_of(p_now, q_after)
            p_now = p_after
        a2[0, 400:440, :] = t2_row(3)
        a2[0, 440:480, :] = t2_row(21)

        def y_level2_of(xb, k):
            e = [a2[xb, pl.ds(k * 40 + j, 18, stride=2), :] for j in range(4)]
            return p_of(e[0], e[1]), q_of(e[2], e[3])

        def y_level2(k):
            place = rows(k * 24, 18)
            for xb in range(2):
                p, q = y_level2_of(xb, k)
                for yb in range(2):
                    value = high_of(p, q) if yb else low_of(p, q)
                    b = 2 * xb + yb
                    if b == 0:
                        e2[pl.ds(k * 24 + 2, 18), :] = value
                    c2[b, place, :] = shrink(old(c2, b, place, slice(None)) + value)

        def y_level2_low(k):
            e2[pl.ds(k * 24 + 2, 18), :] = low_of(*y_level2_of(0, k))

        for k in range(10, 12):
            y_level2_low(k)
        loop(10, y_level2, unroll=10)
        for source, target in ((38, 0), (39, 20)):
            e2[pl.ds(target, 12, stride=24), :] = a2[0, pl.ds(source, 12, stride=40), :]

        t3[...] = times(e2[...], m3)

        def t3_row(i):
            return t3[i * 24 : (i + 1) * 24, :]

        p_now = t3_row(10)
        for k in range(-2, 4):
            if k == 3:
                q_after, p_after = t3_row(11), None
            else:
                even, odd = t3_row(2 * k + 4), t3_row(2 * k + 5)
                q_after, p_after = q_of(even, odd), p_of(even, odd)
            n = (k + 2) * 24
            a3[0, n : n + 24, :] = low_of(p_now, q_after)
            a3[1, n : n + 24, :] = high_of(p_now, q_after)
            p_now = p_after

        lane = lax.broadcasted_iota(jnp.int32, (10, 128), 1)

        def y_level3(k):
            place = rows(k * 16, 10)
            for xb in range(2):
                e = [a3[xb, pl.ds(k * 24 + j, 10, stride=2), :] for j in range(4)]
                p, q = p_of(e[0], e[1]), q_of(e[2], e[3])
                for yb in range(2):
                    value = high_of(p, q) if yb else low_of(p, q)
                    b = 2 * xb + yb
                    value = old(c3, b, place, slice(None)) + value
                    if b == 0:
                        c3[b, place, :] = jnp.where(lane < 32, value, shrink(value))
                    else:
                        c3[b, place, :] = shrink(value)

        loop(6, y_level3, unroll=6)

        def up(low_now, high_now, low_before, high_before):
            p = low_now - RATIO * high_now
            q = high_before + RATIO * low_before
            return p + ROOT_THREE * q, ROOT_THREE * p - q

        for b in range(4):
            s3[b] = times(c3[b], m3t)

        def x_up3(k):
            for yb in range(2):
                e = [s3[b, rows((k + d) * 16, 16), :] for d in (1, 0) for b in (yb, 2 + yb)]
                even, odd = up(*e)
                p3[yb, rows(2 * k * 16, 16), :] = even
                p3[yb, rows((2 * k + 1) * 16, 16), :] = odd

        loop(5, x_up3, unroll=5)

        def y_up3(r):
            e = [p3[b, pl.ds(r * 16 + d, 9), :] for d in (1, 0) for b in (0, 1)]
            even, odd = up(*e)
            d2[pl.ds(r * 24, 9, stride=2), :] = even
            d2[pl.ds(r * 24 + 1, 9, stride=2), :] = odd

        loop(10, y_up3, unroll=10)

        lanes = lax.broadcasted_iota(jnp.int32, (240, 128), 1)
        for b in range(1, 4):
            s2[b] = times(c2[b], m2t)
        s2[0] = times(jnp.where(lanes < 64, d2[...], c2[0]), m2t)

        def x_up2(k):
            for yb in range(2):
                e = [s2[b, rows((k + d) * 24, 24), :] for d in (1, 0) for b in (yb, 2 + yb)]
                even, odd = up(*e)
                p2[yb, rows(2 * k * 24, 24), :] = even
                p2[yb, rows((2 * k + 1) * 24, 24), :] = odd

        loop(9, x_up2, unroll=9)

        def y_up2(r):
            e = [p2[b, pl.ds(r * 24 + d, 17), :] for d in (1, 0) for b in (0, 1)]
            even, odd = up(*e)
            d1[pl.ds(r * 40 + 6, 17, stride=2), :] = even
            d1[pl.ds(r * 40 + 7, 17, stride=2), :] = odd

        loop(18, y_up2, unroll=6)

        wait(i1)
        for tb in range(2):
            halo[tb, 0:32, :] = i1xr[tb * 32 : (tb + 1) * 32, :]
            halo[tb, 32:64, :] = i1xr[(2 + tb) * 32 : (3 + tb) * 32, :]
            halo[tb, 64:80, :] = i1yr[tb * 16 : (tb + 1) * 16, :]
            halo[tb, 80:96, :] = i1yr[(2 + tb) * 16 : (3 + tb) * 16, :]
            halo[tb, 96:97, :] = i1cr[tb : tb + 1, :]
        result = times(jnp.concatenate([halo[0], halo[1]], axis=1), m1t)
        for th in range(2):
            part = result[:, th * 128 : (th + 1) * 128]
            s1[th, 2, 8:40, :] = part[0:32]
            s1[th, 3, 8:40, :] = part[32:64]
            s1[th, 1, pl.ds(47, 16, stride=40), :] = part[64:80]
            s1[th, 3, pl.ds(47, 16, stride=40), :] = part[80:96]
            s1[th, 3, 7:8, :] = part[96:97]

        def time_up1(n):
            place = rows(n * 136, 136)
            lo = d1[rows(40 + n * 136, 136), :]
            result = times(jnp.concatenate([lo, c1[0, place, :]], axis=1), m1t)
            s1[0, 0, place, :] = result[:, :128]
            s1[1, 0, place, :] = result[:, 128:]

        loop(5, time_up1, unroll=5)

        up_parts = [(chunk, th) for chunk in range(4) for th in range(2)]

        def y_up1(row, chunk, th):
            result = []
            for xb in range(2):
                e = [
                    s1[th, 2 * xb + yb, pl.ds(row * 40 + d + 8 * chunk, 8), :]
                    for d in (8, 7) for yb in range(2)
                ]
                result.append(up(*e))
            return [(result[0][n], result[1][n]) for n in range(2)]

        def q_next(low, high):
            return high + RATIO * low

        def up1(k, qs):
            after = []
            n = 0
            for chunk, th in up_parts:
                for parity, (low, high) in enumerate(y_up1(k + 1, chunk, th)):
                    p = low - RATIO * high
                    start = k * 128 + 16 * chunk + parity
                    reb[th, pl.ds(start, 8, stride=2), :] = p + ROOT_THREE * qs[n]
                    reb[th, pl.ds(start + 64, 8, stride=2), :] = ROOT_THREE * p - qs[n]
                    after.append(q_next(low, high))
                    n += 1
            return tuple(after)

        start = tuple(q_next(*one) for chunk, th in up_parts for one in y_up1(0, chunk, th))
        lax.fori_loop(0, 16, up1, start, unroll=2)

    iteration(0)
    iteration(1)

    def finish(r):
        for th in range(2):
            out[r, :, th * 128 : (th + 1) * 128] = reb[th, rows(r * 64, 64), :]

    loop(32, finish, unroll=2)


def solution(mesh):
    nx, ny = mesh.shape["gx"], mesh.shape["gy"]

    def v(*shape):
        return pltpu.VMEM(shape, F32)

    def b(*shape):
        return pltpu.VMEM(shape, BF16)

    scratch = [
        pltpu.VMEM((32, 64, 256), jnp.int32),
        b(768, 256), b(768, 256), b(384, 128), b(384, 128), b(384, 128), b(384, 128),
        v(2, 33 * 72, 128), v(7, 17 * 40, 128), v(22 * 40, 128),
        v(22 * 40, 128), v(2, 12 * 40, 128), v(4, 10 * 24, 128), v(12 * 24, 128),
        v(12 * 24, 128), v(2, 6 * 24, 128), v(4, 6 * 16, 128),
        v(4, 6 * 16, 128), v(2, 10 * 16, 128), v(10 * 24, 128),
        v(4, 10 * 24, 128), v(2, 18 * 24, 128), v(18 * 40, 128),
        v(2, 4, 17 * 40, 128), v(2, 32 * 64, 128), v(2, 104, 128),
        v(2, 64, 128), v(2, 32, 128), v(8, 128), v(2, 32, 128), v(8, 128),
        v(192, 128), v(6, 32, 128), v(2, 192, 128), v(2, 6, 32, 128),
        v(128, 128), v(64, 128), v(8, 128), v(128, 128), v(64, 128), v(8, 128),
        pltpu.SemaphoreType.DMA((1,)), pltpu.SemaphoreType.DMA((28,)), pltpu.SemaphoreType.DMA((28,)),
    ]

    def on_device(counts):
        return pl.pallas_call(
            functools.partial(kernel, nx, ny),
            out_shape=jax.ShapeDtypeStruct(counts.shape, F32),
            in_specs=[pl.BlockSpec(memory_space=pltpu.HBM)],
            out_specs=pl.BlockSpec(memory_space=pltpu.VMEM),
            scratch_shapes=scratch,
            compiler_params=pltpu.CompilerParams(
                collective_id=0, has_side_effects=True, vmem_limit_bytes=50 * 1024 * 1024
            ),
        )(counts)

    spec = P(("grp", "gx"), "gy", None)
    return jax.shard_map(on_device, mesh=mesh, in_specs=(spec,), out_specs=spec, check_vma=False)
```

```python
import functools
import math

import jax
import jax.numpy as jnp
from jax import lax
from jax.experimental import pallas as pl
from jax.experimental.pallas import tpu as pltpu
from jax.sharding import PartitionSpec as P

ROOT_THREE = math.sqrt(3.0)
TAP_SCALE = 4.0 * math.sqrt(2.0)
H = [
    (1.0 + ROOT_THREE) / TAP_SCALE,
    (3.0 + ROOT_THREE) / TAP_SCALE,
    (3.0 - ROOT_THREE) / TAP_SCALE,
    (1.0 - ROOT_THREE) / TAP_SCALE,
]
G = [H[3], -H[2], H[1], -H[0]]
RATIO = 2.0 - ROOT_THREE
SPATIAL_SCALE = H[0] * H[0]
THRESHOLD = 0.1
MESH = pl.DeviceIdType.MESH
F32 = jnp.float32
BF16 = jnp.bfloat16

PLACES = [36, 39, 37, 0, 2, 3, 38]


def shrink(values):
    return values - jnp.clip(values, -THRESHOLD, THRESHOLD)


def p_of(even, odd):
    return even + ROOT_THREE * odd


def q_of(even, odd):
    return ROOT_THREE * even - odd


def q_even(even, odd):
    return even - (1.0 / ROOT_THREE) * odd


def low_of(p, q_after):
    return p + RATIO * q_after


def high_of(p, q_after):
    return q_after - RATIO * p


def loop(count, body, unroll=4):
    def step(i, carry):
        body(i)
        return carry

    lax.fori_loop(0, count, step, 0, unroll=unroll)


def rows(start, size):
    return pl.ds(pl.multiple_of(start, 8), size)


def build_matrix(ref, length, padded, transposed):
    t = lax.broadcasted_iota(jnp.int32, (padded, padded), 1 if transposed else 0)
    c = lax.broadcasted_iota(jnp.int32, (padded, padded), 0 if transposed else 1)
    half = c >= length // 2
    j = (t - 2 * jnp.where(half, c - length // 2, c)) & (length - 1)
    value = jnp.zeros((padded, padded), F32)
    for tap in range(4):
        tap_value = jnp.where(half, G[tap] * SPATIAL_SCALE, H[tap] * SPATIAL_SCALE)
        value = jnp.where(j == tap, tap_value, value)
    if padded > length:
        value = jnp.where((t < length) & (c < length), value, 0.0)
    high = value.astype(BF16)
    low = (value - high.astype(F32)).astype(BF16)
    ref[0:padded, :] = high
    ref[padded : 2 * padded, :] = high
    ref[2 * padded : 3 * padded, :] = low


def times(values, matrix_ref):
    high = values.astype(BF16)
    low = (values - high.astype(F32)).astype(BF16)
    left = jnp.concatenate([high, low, high], axis=1)
    return jnp.dot(left, matrix_ref[...], preferred_element_type=F32)


def functionals(entry, count, level1_q, q_last):
    def low2(i):
        return low_of(p_of(entry(i), entry(i + 1)), q_of(entry(i + 2), entry(i + 3)))

    n = count - 8
    return [
        q_last(entry(0), entry(1)),
        q_last(low2(0), low2(2)),
        level1_q,
        p_of(entry(n + 4), entry(n + 5)),
        entry(n + 6),
        entry(n + 7),
        p_of(low2(n), low2(n + 2)),
    ]


def kernel(
    nx, ny,
    counts_hbm, out, counts, m1, m1t, m2, m2t, m3, m3t,
    t0, c1, e1, t2, a2, c2, e2, t3, a3, c3,
    s3, p3, d2, s2, p2, d1, s1, reb, cb,
    f0q, f0p, f0y, f0qr, f0pr, f0yr,
    f1x, f1y, f1xr, f1yr,
    local_sem, send_sem, recv_sem,
):
    gx = lax.axis_index("gx")
    gy = lax.axis_index("gy")

    def device(dx, dy):
        where = {}
        if dx:
            where["gx"] = lax.rem(gx + dx + nx, nx)
        if dy:
            where["gy"] = lax.rem(gy + dy + ny, ny)
        return where

    load = pltpu.make_async_copy(counts_hbm, counts, local_sem.at[0])
    load.start()

    barrier = pltpu.get_barrier_semaphore()
    around = [(dx, dy) for dx in (-1, 0, 1) for dy in (-1, 0, 1) if dx or dy]
    for dx, dy in around:
        pl.semaphore_signal(barrier, inc=1, device_id=device(dx, dy), device_id_type=MESH)

    def send(first_sem, transfers):
        copies = []
        for n, (source, target, dx, dy) in enumerate(transfers):
            copy = pltpu.make_async_remote_copy(
                src_ref=source,
                dst_ref=target,
                send_sem=send_sem.at[first_sem + n],
                recv_sem=recv_sem.at[first_sem + n],
                device_id=device(dx, dy),
                device_id_type=MESH,
            )
            copy.start()
            copies.append(copy)
        return copies

    def wait(copies):
        for copy in copies:
            copy.wait()

    build_matrix(m1, 256, 256, False)
    build_matrix(m1t, 256, 256, True)
    build_matrix(m2, 128, 128, False)
    build_matrix(m2t, 128, 128, True)
    build_matrix(m3, 64, 128, False)
    build_matrix(m3t, 64, 128, True)
    for ref in (f0q, f0p):
        for tb in range(2):
            ref[tb, 64:72, :] = jnp.zeros((8, 128), F32)
    for ref in (f0qr, f0pr):
        for number in range(2):
            for tb in range(2):
                ref[number, tb, 64:72, :] = jnp.zeros((8, 128), F32)
    for n in range(4):
        f0y[n, 32:40, :] = jnp.zeros((8, 128), F32)
        for place in (1, 35):
            cb[n, place : place + 1, :] = jnp.zeros((1, 128), F32)
    for tb in range(2):
        t0[tb, pl.ds(65, 32, stride=72), :] = jnp.zeros((32, 128), F32)
    for place in (1, 21):
        e2[pl.ds(place, 12, stride=24), :] = jnp.zeros((12, 128), F32)
    e1[...] = jnp.zeros((960, 128), F32)
    f1y[...] = jnp.zeros((7, 40, 128), F32)
    load.wait()

    def residual(count, rebuilt):
        observed = count.astype(F32) * (1.0 / 64.0)
        weight = 1.0 / (1.0 + jnp.abs(observed))
        if rebuilt is None:
            return weight * observed
        return weight * (observed - rebuilt)

    def iteration(number):
        first = number == 0
        sem = 12 * number

        def old(ref, *index):
            return 0.0 if first else ref[index]

        def time_rows(n):
            count = counts[pl.ds(n * 4, 4)].reshape(256, 256)
            if first:
                values = residual(count, None)
            else:
                rebuilt = jnp.concatenate(
                    [reb[0, rows(n * 256, 256), :], reb[1, rows(n * 256, 256), :]], axis=1
                )
                values = residual(count, rebuilt)
            result = times(values, m1)
            for i in range(4):
                for tb in range(2):
                    t0[tb, rows((n * 4 + i) * 72, 64), :] = result[
                        i * 64 : (i + 1) * 64, tb * 128 : (tb + 1) * 128
                    ]

        loop(8, time_rows)

        qr, pr, cr = f0qr.at[number], f0pr.at[number], f0yr.at[number]
        xr, yr = f1xr.at[number], f1yr.at[number]
        for tb in range(2):
            f0q[tb, 0:64, :] = q_of(t0[tb, 0:64, :], t0[tb, 72:136, :])
            f0p[tb, 0:64, :] = p_of(t0[tb, 2160:2224, :], t0[tb, 2232:2296, :])
            column = [t0[tb, pl.ds(y, 32, stride=72), :] for y in (0, 1, 62, 63)]
            f0y[tb, 0:32, :] = q_even(column[0], column[1])
            f0y[2 + tb, 0:32, :] = p_of(column[2], column[3])
            for block, source in ((27, f0q), (36, f0p)):
                f1y[tb, block : block + 1, :] = q_even(source[tb, 0:1, :], source[tb, 1:2, :])
                f1y[3 + tb, block : block + 1, :] = p_of(source[tb, 62:63, :], source[tb, 63:64, :])
        t0[0, pl.ds(64, 32, stride=72), :] = jnp.zeros((32, 128), F32)

        def y_low(read):
            e = [read(j) for j in range(4)]
            return low_of(p_of(e[0], e[1]), q_of(e[2], e[3]))

        def low_pair(k):
            return [
                [
                    y_low(lambda j: t0[0, pl.ds((2 * k + i) * 72 + 16 * chunk + j, 8, stride=2), :])
                    for i in range(2)
                ]
                for chunk in range(4)
            ]

        def low_store(k, chunk, value):
            e1[pl.ds((k + 4) * 40 + 4 + 8 * chunk, 8), :] = value

        def low_step(k, ps):
            after = low_pair(k + 1)
            for chunk in range(4):
                low_store(k, chunk, low_of(ps[chunk], q_of(*after[chunk])))
            return tuple(p_of(*one) for one in after)

        ps = lax.fori_loop(0, 15, low_step, tuple(p_of(*one) for one in low_pair(0)), unroll=5)
        for chunk in range(4):
            low_store(15, chunk, ps[chunk])
            low_store(19, chunk, y_low(lambda j: f0q[0, pl.ds(16 * chunk + j, 8, stride=2), :]))
        e1[pl.ds(161, 16, stride=40), :] = ROOT_THREE * y_low(lambda j: f0y[0, pl.ds(j, 16, stride=2), :])
        e1[921:922, :] = q_of(f0q[0, 0:1, :], f0q[0, 1:2, :])

        for base, part in ((0, slice(4, 36)), (1, slice(1, 2))):

            def entry(i):
                return e1[i * 40 + part.start : i * 40 + part.stop, :]

            values = functionals(lambda i: entry(4 + i), 16, entry(23), q_of)
            for n, value in enumerate(values):
                tile = 0 if n < 3 else 104
                n = n if n < 3 else n - 3
                start = tile + n if base else tile + 8 + 32 * n
                f1x[start : start + (1 if base else 32), :] = value
        for source, base, size, stride, level1_q, target in (
            (e1, 164, 16, 40, pl.ds(161, 16, stride=40), 0),
            (e1, 924, 1, 1, pl.ds(921, 1), 16),
            (f1x, 8, 3, 32, pl.ds(0, 3), 24),
            (f1x, 112, 4, 32, pl.ds(104, 4), 32),
        ):

            def entry(i):
                return source[pl.ds(base + i, size, stride=stride) if size > 1 else pl.ds(base + i, 1), :]

            for n, value in enumerate(functionals(entry, 32, source[level1_q, :], q_even)):
                f1y[n, target : target + size, :] = value
        if first:
            pl.semaphore_wait(barrier, 8)
        f1 = send(sem + 4, [
            (f1x.at[0:104], xr.at[0:104], -1, 0),
            (f1x.at[104:240], xr.at[104:240], 1, 0),
            (f1y.at[0:3, 0:24], yr.at[0:3, 0:24], 0, -1),
            (f1y.at[3:7, 0:24], yr.at[3:7, 0:24], 0, 1),
            (f1y.at[0:3, 24:32], yr.at[0:3, 24:32], -1, -1),
            (f1y.at[3:7, 24:32], yr.at[3:7, 24:32], -1, 1),
            (f1y.at[0:3, 32:40], yr.at[0:3, 32:40], 1, -1),
            (f1y.at[3:7, 32:40], yr.at[3:7, 32:40], 1, 1),
        ])

        f0 = send(sem, [
            (f0q.at[:, 0:64], qr.at[:, 0:64], -1, 0),
            (f0p.at[:, 0:64], pr.at[:, 0:64], 1, 0),
            (f0y.at[0:2], cr.at[0:2], 0, -1),
            (f0y.at[2:4], cr.at[2:4], 0, 1),
        ])

        def y_level1(read):
            e = [read(j) for j in range(4)]
            p, q = p_of(e[0], e[1]), q_of(e[2], e[3])
            return [low_of(p, q), high_of(p, q)]

        def y_own(row, chunk, tb):
            return y_level1(lambda j: t0[tb, pl.ds(row * 72 + 16 * chunk + j, 8, stride=2), :])

        def y_halo(ref, chunk, tb):
            return y_level1(lambda j: ref[tb, pl.ds(16 * chunk + j, 8, stride=2), :])

        def level1_store(k, chunk, tb, yb, p, q):
            for xb in range(2):
                band = 4 * xb + 2 * yb + tb
                if band:
                    value = high_of(p, q) if xb else low_of(p, q)
                    place = rows((k + 1) * 40 + 8 + 8 * chunk, 8)
                    c1[band - 1, place, :] = shrink(old(c1, band - 1, place, slice(None)) + value)

        def pair(k, parts):
            result = []
            for chunk, tb in parts:
                first_row, second_row = y_own(2 * k, chunk, tb), y_own(2 * k + 1, chunk, tb)
                result += [(first_row[yb], second_row[yb]) for yb in range(2)]
            return result

        def store_all(k, parts, ps, qs):
            for n, (chunk, tb) in enumerate(parts):
                for yb in range(2):
                    level1_store(k, chunk, tb, yb, ps[2 * n + yb], qs[2 * n + yb])

        def level1(parts):
            def step(k, ps):
                after = pair(k + 1, parts)
                store_all(k, parts, ps, [q_of(*one) for one in after])
                return tuple(p_of(*one) for one in after)

            return lax.fori_loop(0, 15, step, tuple(p_of(*one) for one in pair(0, parts)), unroll=3)

        def level1_ends(parts, last):
            before = [value for part in parts for value in y_halo(pr, *part)]
            store_all(-1, parts, before, [q_of(*one) for one in pair(0, parts)])
            store_all(15, parts, last, [value for part in parts for value in y_halo(qr, *part)])

        inner = [(chunk, tb) for chunk in range(3) for tb in range(2)]
        edge = [(3, tb) for tb in range(2)]
        inner_last = level1(inner)

        def time_up1_pieces(pieces):
            for b in range(1, 4):
                values = jnp.concatenate(
                    [
                        jnp.concatenate([c1[band, start:stop, :] for start, stop in pieces], axis=0)
                        for band in (2 * b - 1, 2 * b)
                    ],
                    axis=1,
                )
                result = times(values, m1t)
                n = 0
                for start, stop in pieces:
                    for th in range(2):
                        s1[th, b, start:stop, :] = result[n : n + stop - start, th * 128 : (th + 1) * 128]
                    n += stop - start

        time_up1_pieces([(row * 40 + 8, row * 40 + 32) for row in range(1, 16)])
        wait(f1)

        for tile, first_row, count in ((0, 20, 3), (104, 0, 4)):
            e1[pl.ds(first_row * 40 + 1, count, stride=40), :] = xr[tile : tile + count, :]
            for n in range(count):
                row = (first_row + n) * 40
                e1[row + 4 : row + 36, :] = xr[tile + 8 + 32 * n : tile + 40 + 32 * n, :]
        for n, place in enumerate(PLACES):
            e1[pl.ds(160 + place, 16, stride=40), :] = yr[n, 0:16, :]
            e1[pl.ds(920 + place, 1), :] = yr[n, 16:17, :]
            e1[pl.ds(800 + place, 3, stride=40), :] = yr[n, 24:27, :]
            e1[pl.ds(place, 4, stride=40), :] = yr[n, 32:36, :]
        for target, source in ((19, 22), (2, 23)):
            e1[target * 40 : (target + 1) * 40, :] += RATIO * e1[source * 40 : (source + 1) * 40, :]
        for target, source in ((35, 37), (3, 1)):
            place = pl.ds(target, 22, stride=40)
            e1[place, :] = e1[place, :] + RATIO * e1[pl.ds(source, 22, stride=40), :]
        for place in (1, 37):
            e1[pl.ds(place, 22, stride=40), :] = jnp.zeros((22, 128), F32)

        def time_level2(n):
            t2[rows(n * 176, 176), :] = times(e1[rows(n * 176, 176), :], m2)

        loop(5, time_level2, unroll=5)

        def t2_row(i):
            return t2[i * 40 : (i + 1) * 40, :]

        p_now, q_after = t2_row(0), None
        for k in range(-2, 8):
            if k == 7:
                q_after, p_after = t2_row(20), None
            else:
                m = 1 if k == -2 else 6 + 2 * k
                even, odd = t2_row(m), t2_row(m + 1)
                q_after, p_after = q_of(even, odd), p_of(even, odd)
            n = (k + 2) * 40
            a2[0, n : n + 40, :] = low_of(p_now, q_after)
            a2[1, n : n + 40, :] = high_of(p_now, q_after)
            p_now = p_after
        a2[0, 400:440, :] = t2_row(3)
        a2[0, 440:480, :] = t2_row(21)

        def y_level2_of(xb, k):
            e = [a2[xb, pl.ds(k * 40 + j, 18, stride=2), :] for j in range(4)]
            return p_of(e[0], e[1]), q_of(e[2], e[3])

        def y_level2(k):
            place = rows(k * 24, 18)
            for xb in range(2):
                p, q = y_level2_of(xb, k)
                for yb in range(2):
                    value = high_of(p, q) if yb else low_of(p, q)
                    b = 2 * xb + yb
                    if b == 0:
                        e2[pl.ds(k * 24 + 2, 18), :] = value
                    c2[b, place, :] = shrink(old(c2, b, place, slice(None)) + value)

        def y_level2_low(k):
            e2[pl.ds(k * 24 + 2, 18), :] = low_of(*y_level2_of(0, k))

        for k in range(10, 12):
            y_level2_low(k)
        loop(10, y_level2, unroll=10)
        for source, target in ((38, 0), (39, 20)):
            e2[pl.ds(target, 12, stride=24), :] = a2[0, pl.ds(source, 12, stride=40), :]

        t3[...] = times(e2[...], m3)

        def t3_row(i):
            return t3[i * 24 : (i + 1) * 24, :]

        p_now = t3_row(10)
        for k in range(-2, 4):
            if k == 3:
                q_after, p_after = t3_row(11), None
            else:
                even, odd = t3_row(2 * k + 4), t3_row(2 * k + 5)
                q_after, p_after = q_of(even, odd), p_of(even, odd)
            n = (k + 2) * 24
            a3[0, n : n + 24, :] = low_of(p_now, q_after)
            a3[1, n : n + 24, :] = high_of(p_now, q_after)
            p_now = p_after

        lane = lax.broadcasted_iota(jnp.int32, (10, 128), 1)

        def y_level3(k):
            place = rows(k * 16, 10)
            for xb in range(2):
                e = [a3[xb, pl.ds(k * 24 + j, 10, stride=2), :] for j in range(4)]
                p, q = p_of(e[0], e[1]), q_of(e[2], e[3])
                for yb in range(2):
                    value = high_of(p, q) if yb else low_of(p, q)
                    b = 2 * xb + yb
                    value = old(c3, b, place, slice(None)) + value
                    if b == 0:
                        c3[b, place, :] = jnp.where(lane < 32, value, shrink(value))
                    else:
                        c3[b, place, :] = shrink(value)

        loop(6, y_level3, unroll=6)

        def up(low_now, high_now, low_before, high_before):
            p = low_now - RATIO * high_now
            q = high_before + RATIO * low_before
            return p + ROOT_THREE * q, ROOT_THREE * p - q

        for b in range(4):
            s3[b] = times(c3[b], m3t)

        def x_up3(k):
            for yb in range(2):
                e = [s3[b, rows((k + d) * 16, 16), :] for d in (1, 0) for b in (yb, 2 + yb)]
                even, odd = up(*e)
                p3[yb, rows(2 * k * 16, 16), :] = even
                p3[yb, rows((2 * k + 1) * 16, 16), :] = odd

        loop(5, x_up3, unroll=5)

        def y_up3(r):
            e = [p3[b, pl.ds(r * 16 + d, 9), :] for d in (1, 0) for b in (0, 1)]
            even, odd = up(*e)
            d2[pl.ds(r * 24, 9, stride=2), :] = even
            d2[pl.ds(r * 24 + 1, 9, stride=2), :] = odd

        loop(10, y_up3, unroll=10)

        lanes = lax.broadcasted_iota(jnp.int32, (240, 128), 1)
        for b in range(1, 4):
            s2[b] = times(c2[b], m2t)
        s2[0] = times(jnp.where(lanes < 64, d2[...], c2[0]), m2t)

        def x_up2(k):
            for yb in range(2):
                e = [s2[b, rows((k + d) * 24, 24), :] for d in (1, 0) for b in (yb, 2 + yb)]
                even, odd = up(*e)
                p2[yb, rows(2 * k * 24, 24), :] = even
                p2[yb, rows((2 * k + 1) * 24, 24), :] = odd

        loop(9, x_up2, unroll=9)

        def y_up2(r):
            e = [p2[b, pl.ds(r * 24 + d, 17), :] for d in (1, 0) for b in (0, 1)]
            even, odd = up(*e)
            d1[pl.ds(r * 40 + 6, 17, stride=2), :] = even
            d1[pl.ds(r * 40 + 7, 17, stride=2), :] = odd

        loop(18, y_up2, unroll=6)

        wait(f0)
        for tb in range(2):
            t0[tb, pl.ds(64, 32, stride=72), :] = cr[tb, 0:32, :]
            qr[tb, 64:65, :] = yr[tb, 27:28, :]
            pr[tb, 64:65, :] = yr[tb, 36:37, :]
            for place, p, q, scale in (
                (pl.ds(2, 32), cr[2 + tb, 0:32, :], ROOT_THREE * f0y[tb, 0:32, :], 1.0),
                (pl.ds(0, 1), yr[3 + tb, 36:37, :], q_of(pr[tb, 0:1, :], pr[tb, 1:2, :]), 1.0),
                (pl.ds(34, 1), yr[3 + tb, 27:28, :], q_of(qr[tb, 0:1, :], qr[tb, 1:2, :]), 1.0 / ROOT_THREE),
            ):
                cb[tb, place, :] = scale * low_of(p, q)
                cb[2 + tb, place, :] = scale * high_of(p, q)
        level1_ends(inner, inner_last)
        level1_ends(edge, level1(edge))
        for yb in range(2):
            for tb in range(2):
                e = [cb[2 * yb + tb, pl.ds(j, 17, stride=2), :] for j in range(4)]
                p, q = p_of(e[0], e[1]), q_of(e[2], e[3])
                for xb in range(2):
                    band = 4 * xb + 2 * yb + tb
                    if band:
                        value = high_of(p, q) if xb else low_of(p, q)
                        place = pl.ds(7, 17, stride=40)
                        c1[band - 1, place, :] = shrink(old(c1, band - 1, place, slice(None)) + value)

        time_up1_pieces([(0, 40), (640, 680)] + [(row * 40 + y, row * 40 + y + 8) for row in range(1, 16) for y in (0, 32)])

        def time_up1(n):
            place = rows(n * 136, 136)
            lo = d1[rows(40 + n * 136, 136), :]
            result = times(jnp.concatenate([lo, c1[0, place, :]], axis=1), m1t)
            s1[0, 0, place, :] = result[:, :128]
            s1[1, 0, place, :] = result[:, 128:]

        loop(5, time_up1, unroll=5)

        up_parts = [(chunk, th) for chunk in range(4) for th in range(2)]

        def y_up1(row, chunk, th):
            result = []
            for xb in range(2):
                e = [
                    s1[th, 2 * xb + yb, pl.ds(row * 40 + d + 8 * chunk, 8), :]
                    for d in (8, 7) for yb in range(2)
                ]
                result.append(up(*e))
            return [(result[0][n], result[1][n]) for n in range(2)]

        def q_next(low, high):
            return high + RATIO * low

        def up1(k, qs):
            after = []
            n = 0
            for chunk, th in up_parts:
                for parity, (low, high) in enumerate(y_up1(k + 1, chunk, th)):
                    p = low - RATIO * high
                    start = k * 128 + 16 * chunk + parity
                    reb[th, pl.ds(start, 8, stride=2), :] = p + ROOT_THREE * qs[n]
                    reb[th, pl.ds(start + 64, 8, stride=2), :] = ROOT_THREE * p - qs[n]
                    after.append(q_next(low, high))
                    n += 1
            return tuple(after)

        start = tuple(q_next(*one) for chunk, th in up_parts for one in y_up1(0, chunk, th))
        lax.fori_loop(0, 16, up1, start, unroll=2)

    iteration(0)
    iteration(1)

    def finish(r):
        for th in range(2):
            out[r, :, th * 128 : (th + 1) * 128] = reb[th, rows(r * 64, 64), :]

    loop(32, finish, unroll=2)


def solution(mesh):
    nx, ny = mesh.shape["gx"], mesh.shape["gy"]

    def v(*shape):
        return pltpu.VMEM(shape, F32)

    def b(*shape):
        return pltpu.VMEM(shape, BF16)

    scratch = [
        pltpu.VMEM((32, 64, 256), jnp.int32),
        b(768, 256), b(768, 256), b(384, 128), b(384, 128), b(384, 128), b(384, 128),
        v(2, 32 * 72, 128), v(7, 17 * 40, 128), v(24 * 40, 128),
        v(22 * 40, 128), v(2, 12 * 40, 128), v(4, 10 * 24, 128), v(12 * 24, 128),
        v(12 * 24, 128), v(2, 6 * 24, 128), v(4, 6 * 16, 128),
        v(4, 6 * 16, 128), v(2, 10 * 16, 128), v(10 * 24, 128),
        v(4, 10 * 24, 128), v(2, 18 * 24, 128), v(18 * 40, 128),
        v(2, 4, 17 * 40, 128), v(2, 32 * 64, 128), v(4, 40, 128),
        v(2, 72, 128), v(2, 72, 128), v(4, 40, 128), v(2, 2, 72, 128), v(2, 2, 72, 128), v(2, 4, 40, 128),
        v(240, 128), v(7, 40, 128), v(2, 240, 128), v(2, 7, 40, 128),
        pltpu.SemaphoreType.DMA((1,)), pltpu.SemaphoreType.DMA((24,)), pltpu.SemaphoreType.DMA((24,)),
    ]

    def on_device(counts):
        return pl.pallas_call(
            functools.partial(kernel, nx, ny),
            out_shape=jax.ShapeDtypeStruct(counts.shape, F32),
            in_specs=[pl.BlockSpec(memory_space=pltpu.HBM)],
            out_specs=pl.BlockSpec(memory_space=pltpu.VMEM),
            scratch_shapes=scratch,
            compiler_params=pltpu.CompilerParams(
                collective_id=0, has_side_effects=True, vmem_limit_bytes=50 * 1024 * 1024
            ),
        )(counts)

    spec = P(("grp", "gx"), "gy", None)
    return jax.shard_map(on_device, mesh=mesh, in_specs=(spec,), out_specs=spec, check_vma=False)
```

```python
import functools
import math

import jax
import jax.numpy as jnp
from jax import lax
from jax.experimental import pallas as pl
from jax.experimental.pallas import tpu as pltpu
from jax.sharding import PartitionSpec as P

ROOT_THREE = math.sqrt(3.0)
TAP_SCALE = 4.0 * math.sqrt(2.0)
H = [
    (1.0 + ROOT_THREE) / TAP_SCALE,
    (3.0 + ROOT_THREE) / TAP_SCALE,
    (3.0 - ROOT_THREE) / TAP_SCALE,
    (1.0 - ROOT_THREE) / TAP_SCALE,
]
G = [H[3], -H[2], H[1], -H[0]]
RATIO = 2.0 - ROOT_THREE
SPATIAL_SCALE = H[0] * H[0]
THRESHOLD = 0.1
MESH = pl.DeviceIdType.MESH
F32 = jnp.float32
BF16 = jnp.bfloat16

PLACES = [36, 39, 37, 0, 2, 3, 38]
CORNERS = [((-1, -1), 9), ((-1, 1), 12), ((1, -1), 12), ((1, 1), 16)]


def shrink(values):
    return values - jnp.clip(values, -THRESHOLD, THRESHOLD)


def p_of(even, odd):
    return even + ROOT_THREE * odd


def q_of(even, odd):
    return ROOT_THREE * even - odd


def q_even(even, odd):
    return even - (1.0 / ROOT_THREE) * odd


def low_of(p, q_after):
    return p + RATIO * q_after


def high_of(p, q_after):
    return q_after - RATIO * p


def loop(count, body, unroll=4):
    def step(i, carry):
        body(i)
        return carry

    lax.fori_loop(0, count, step, 0, unroll=unroll)


def rows(start, size):
    return pl.ds(pl.multiple_of(start, 8), size)


def build_matrix(ref, length, padded, transposed):
    t = lax.broadcasted_iota(jnp.int32, (padded, padded), 1 if transposed else 0)
    c = lax.broadcasted_iota(jnp.int32, (padded, padded), 0 if transposed else 1)
    half = c >= length // 2
    j = (t - 2 * jnp.where(half, c - length // 2, c)) & (length - 1)
    value = jnp.zeros((padded, padded), F32)
    for tap in range(4):
        tap_value = jnp.where(half, G[tap] * SPATIAL_SCALE, H[tap] * SPATIAL_SCALE)
        value = jnp.where(j == tap, tap_value, value)
    if padded > length:
        value = jnp.where((t < length) & (c < length), value, 0.0)
    high = value.astype(BF16)
    low = (value - high.astype(F32)).astype(BF16)
    ref[0:padded, :] = high
    ref[padded : 2 * padded, :] = high
    ref[2 * padded : 3 * padded, :] = low


def times(values, matrix_ref):
    high = values.astype(BF16)
    low = (values - high.astype(F32)).astype(BF16)
    left = jnp.concatenate([high, low, high], axis=1)
    return jnp.dot(left, matrix_ref[...], preferred_element_type=F32)


def functionals(entry, count, level1_q, q_last):
    def low2(i):
        return low_of(p_of(entry(i), entry(i + 1)), q_of(entry(i + 2), entry(i + 3)))

    n = count - 8
    return [
        q_last(entry(0), entry(1)),
        q_last(low2(0), low2(2)),
        level1_q,
        p_of(entry(n + 4), entry(n + 5)),
        entry(n + 6),
        entry(n + 7),
        p_of(low2(n), low2(n + 2)),
    ]


def kernel(
    nx, ny,
    counts_hbm, out, counts, m1, m1t, m2, m2t, m3, m3t,
    t0, c1, e1, t2, a2, c2, e2, t3, a3, c3,
    s3, p3, d2, s2, p2, d1, s1, reb, cb,
    f0q, f0p, fq, fp, f0y, f0qr, f0pr, f0yr,
    f1x, f1y, f1xr, f1yr, fc, fcr,
    local_sem, send_sem, recv_sem,
):
    gx = lax.axis_index("gx")
    gy = lax.axis_index("gy")

    def device(dx, dy):
        where = {}
        if dx:
            where["gx"] = lax.rem(gx + dx + nx, nx)
        if dy:
            where["gy"] = lax.rem(gy + dy + ny, ny)
        return where

    load = pltpu.make_async_copy(counts_hbm, counts, local_sem.at[0])
    load.start()

    barrier = pltpu.get_barrier_semaphore()
    around = [(dx, dy) for dx in (-1, 0, 1) for dy in (-1, 0, 1) if dx or dy]
    for dx, dy in around:
        pl.semaphore_signal(barrier, inc=1, device_id=device(dx, dy), device_id_type=MESH)

    def send(first_sem, transfers):
        copies = []
        for n, (source, target, dx, dy) in enumerate(transfers):
            copy = pltpu.make_async_remote_copy(
                src_ref=source,
                dst_ref=target,
                send_sem=send_sem.at[first_sem + n],
                recv_sem=recv_sem.at[first_sem + n],
                device_id=device(dx, dy),
                device_id_type=MESH,
            )
            copy.start()
            copies.append(copy)
        return copies

    def wait(copies):
        for copy in copies:
            copy.wait()

    build_matrix(m1, 256, 256, False)
    for ref in (f0q, f0p):
        for tb in range(2):
            ref[tb, 64:72, :] = jnp.zeros((8, 128), F32)
    for n in range(4):
        f0y[n, 32:40, :] = jnp.zeros((8, 128), F32)
        for place in (1, 35):
            cb[n, place : place + 1, :] = jnp.zeros((1, 128), F32)
    for tb in range(2):
        t0[tb, pl.ds(65, 32, stride=72), :] = jnp.zeros((32, 128), F32)
    for place in (1, 21):
        e2[pl.ds(place, 12, stride=24), :] = jnp.zeros((12, 128), F32)
    e1[...] = jnp.zeros((960, 128), F32)
    f1y[...] = jnp.zeros((7, 24, 128), F32)
    load.wait()

    def residual(count, rebuilt):
        observed = count.astype(F32) * (1.0 / 64.0)
        weight = 1.0 / (1.0 + jnp.abs(observed))
        if rebuilt is None:
            return weight * observed
        return weight * (observed - rebuilt)

    def iteration(number, synthesis):
        first = number == 0
        sem = 12 * number

        def old(ref, *index):
            return 0.0 if first else ref[index]

        qr, pr, cr = f0qr.at[number], f0pr.at[number], f0yr.at[number]
        xr, yr = f1xr.at[number], f1yr.at[number]

        def time_rows(n):
            count = counts[pl.ds(n * 4, 4)].reshape(256, 256)
            if first:
                values = residual(count, None)
            else:
                rebuilt = jnp.concatenate(
                    [reb[0, rows(n * 256, 256), :], reb[1, rows(n * 256, 256), :]], axis=1
                )
                values = residual(count, rebuilt)
            result = times(values, m1)
            for i in range(4):
                for tb in range(2):
                    t0[tb, rows((n * 4 + i) * 72, 64), :] = result[
                        i * 64 : (i + 1) * 64, tb * 128 : (tb + 1) * 128
                    ]

        t0[0, pl.ds(64, 32, stride=72), :] = jnp.zeros((32, 128), F32)

        def y_low(read):
            e = [read(j) for j in range(4)]
            return low_of(p_of(e[0], e[1]), q_of(e[2], e[3]))

        def low_pair(k):
            return [
                [
                    y_low(lambda j: t0[0, pl.ds((2 * k + i) * 72 + 16 * chunk + j, 8, stride=2), :])
                    for i in range(2)
                ]
                for chunk in range(4)
            ]

        def low_store(k, chunk, value):
            e1[pl.ds((k + 4) * 40 + 4 + 8 * chunk, 8), :] = value

        def low_band(first_k, count):
            def low_step(n, ps):
                k = first_k + n
                after = low_pair(k + 1)
                for chunk in range(4):
                    low_store(k, chunk, low_of(ps[chunk], q_of(*after[chunk])))
                return tuple(p_of(*one) for one in after)

            ps = tuple(p_of(*one) for one in low_pair(first_k))
            return lax.fori_loop(0, count, low_step, ps, unroll=4)

        def y_level1_q(places):
            e1[pl.ds(161 + 40 * places, 8, stride=40), :] = ROOT_THREE * y_low(
                lambda j: f0y[0, pl.ds(2 * places + j, 8, stride=2), :]
            )

        def x_functionals(kind):
            for base, part in ((0, slice(4, 36)), (1, slice(1, 2))):

                def entry(i):
                    return e1[i * 40 + part.start : i * 40 + part.stop, :]

                values = functionals(lambda i: entry(4 + i), 16, entry(23), q_of)
                for n, value in enumerate(values[3:] if kind else values[:3]):
                    tile = 104 * kind
                    start = tile + n if base else tile + 8 + 32 * n
                    f1x[start : start + (1 if base else 32), :] = value

        def half(number_of_half):
            if synthesis is not None:
                synthesis(8 * number_of_half)
            loop(4, lambda n: time_rows(n + 4 * number_of_half))
            start = 16 * number_of_half * 72
            for tb in range(2):
                column = [t0[tb, pl.ds(start + y, 16, stride=72), :] for y in (0, 1, 62, 63)]
                place = pl.ds(16 * number_of_half, 16)
                f0y[tb, place, :] = q_even(column[0], column[1])
                f0y[2 + tb, place, :] = p_of(column[2], column[3])
                if number_of_half:
                    f0p[tb, 0:64, :] = p_of(t0[tb, 2160:2224, :], t0[tb, 2232:2296, :])
                else:
                    f0q[tb, 0:64, :] = q_of(t0[tb, 0:64, :], t0[tb, 72:136, :])

        half(1)
        ps = low_band(8, 7)
        for chunk in range(4):
            low_store(15, chunk, ps[chunk])
        y_level1_q(8)
        x_functionals(1)
        x_after = [(f1x.at[104:240], xr.at[104:240], 1, 0)]
        if not first:
            f1 = send(sem + 4, x_after)

        half(0)
        low_band(0, 8)
        for chunk in range(4):
            low_store(19, chunk, y_low(lambda j: f0q[0, pl.ds(16 * chunk + j, 8, stride=2), :]))
        y_level1_q(0)
        e1[921:922, :] = q_of(f0q[0, 0:1, :], f0q[0, 1:2, :])
        x_functionals(0)

        for tb in range(2):
            for n, source in ((0, f0q), (2, f0p)):
                place = slice(CORNERS[n][1] + tb, CORNERS[n][1] + tb + 1)
                fc[n, place, :] = q_even(source[tb, 0:1, :], source[tb, 1:2, :])
                place = slice(CORNERS[n + 1][1] + tb, CORNERS[n + 1][1] + tb + 1)
                fc[n + 1, place, :] = p_of(source[tb, 62:63, :], source[tb, 63:64, :])
        for source, base, size, stride, level1_q, target in (
            (e1, 164, 16, 40, pl.ds(161, 16, stride=40), 0),
            (e1, 924, 1, 1, pl.ds(921, 1), 16),
            (f1x, 8, 3, 32, pl.ds(0, 3), None),
            (f1x, 112, 4, 32, pl.ds(104, 4), None),
        ):

            def entry(i):
                return source[pl.ds(base + i, size, stride=stride) if size > 1 else pl.ds(base + i, 1), :]

            for n, value in enumerate(functionals(entry, 32, source[level1_q, :], q_even)):
                if target is None:
                    corner, start = 2 * (size - 3) + (n > 2), (n - 3 * (n > 2)) * size
                    fc[corner, start : start + size, :] = value
                else:
                    f1y[n, target : target + size, :] = value
        if first:
            pl.semaphore_wait(barrier, 8)
        f1 = ([] if first else f1) + send(sem + 5, [
            (fc.at[n, 0 : used + 2], fcr.at[number, n, 0 : used + 2], dx, dy)
            for n, ((dx, dy), used) in enumerate(CORNERS)
        ] + [
            (f1x.at[0:104], xr.at[0:104], -1, 0),
            (f1y.at[0:3], yr.at[0:3], 0, -1),
            (f1y.at[3:7], yr.at[3:7], 0, 1),
        ])
        if first:
            f1 += send(sem + 4, x_after)

        def y_level1(read):
            e = [read(j) for j in range(4)]
            p, q = p_of(e[0], e[1]), q_of(e[2], e[3])
            return [low_of(p, q), high_of(p, q)]

        def y_halo(ref, chunk, tb):
            return y_level1(lambda j: ref[tb, pl.ds(16 * chunk + j, 8, stride=2), :])

        for source, target in ((f0q, fq), (f0p, fp)):
            for chunk in range(4):
                for n, value in enumerate(y_halo(source, chunk, 1) + y_halo(source, chunk, 0)[1:]):
                    target[32 * n + 8 * chunk : 32 * n + 8 * chunk + 8, :] = value
            target[96:97, :] = q_of(source[1, 0:1, :], source[1, 1:2, :])
        f0 = send(sem, [
            (fq.at[0:97], qr.at[0:97], -1, 0),
            (fp.at[0:97], pr.at[0:97], 1, 0),
            (f0y.at[0:2], cr.at[0:2], 0, -1),
            (f0y.at[2:4], cr.at[2:4], 0, 1),
        ])

        if first:
            build_matrix(m1t, 256, 256, True)
            build_matrix(m2, 128, 128, False)
            build_matrix(m2t, 128, 128, True)
            build_matrix(m3, 64, 128, False)
            build_matrix(m3t, 64, 128, True)

        def y_own(row, chunk, tb):
            return y_level1(lambda j: t0[tb, pl.ds(row * 72 + 16 * chunk + j, 8, stride=2), :])

        def level1_store(k, chunk, tb, yb, p, q):
            for xb in range(2):
                band = 4 * xb + 2 * yb + tb
                if band:
                    value = high_of(p, q) if xb else low_of(p, q)
                    place = rows((k + 1) * 40 + 8 + 8 * chunk, 8)
                    c1[band - 1, place, :] = shrink(old(c1, band - 1, place, slice(None)) + value)

        def pair(k, parts):
            result = []
            for chunk, tb in parts:
                first_row, second_row = y_own(2 * k, chunk, tb), y_own(2 * k + 1, chunk, tb)
                result += [(first_row[yb], second_row[yb]) for yb in range(2)]
            return result

        def store_all(k, parts, ps, qs):
            for n, (chunk, tb) in enumerate(parts):
                for yb in range(2):
                    level1_store(k, chunk, tb, yb, ps[2 * n + yb], qs[2 * n + yb])

        def level1(parts):
            def step(k, ps):
                after = pair(k + 1, parts)
                store_all(k, parts, ps, [q_of(*one) for one in after])
                return tuple(p_of(*one) for one in after)

            return lax.fori_loop(0, 15, step, tuple(p_of(*one) for one in pair(0, parts)), unroll=3)

        def received(ref, low_row, chunk, tb):
            if tb:
                return [ref[32 * yb + 8 * chunk : 32 * yb + 8 * chunk + 8, :] for yb in range(2)]
            place = low_row + 8 * chunk
            return [xr[place : place + 8, :], ref[64 + 8 * chunk : 72 + 8 * chunk, :]]

        def level1_ends(parts, last):
            before = [value for part in parts for value in received(pr, 176, *part)]
            store_all(-1, parts, before, [q_of(*one) for one in pair(0, parts)])
            store_all(15, parts, last, [value for part in parts for value in received(qr, 72, *part)])

        inner = [(chunk, tb) for chunk in range(3) for tb in range(2)]
        edge = [(3, tb) for tb in range(2)]
        inner_last = level1(inner)

        def time_up1_pieces(pieces):
            for b in range(1, 4):
                values = jnp.concatenate(
                    [
                        jnp.concatenate([c1[band, start:stop, :] for start, stop in pieces], axis=0)
                        for band in (2 * b - 1, 2 * b)
                    ],
                    axis=1,
                )
                result = times(values, m1t)
                n = 0
                for start, stop in pieces:
                    for th in range(2):
                        s1[th, b, start:stop, :] = result[n : n + stop - start, th * 128 : (th + 1) * 128]
                    n += stop - start

        time_up1_pieces([(row * 40 + 8, row * 40 + 32) for row in range(1, 16)])
        wait(f1)

        for tile, first_row, count in ((0, 20, 3), (104, 0, 4)):
            e1[pl.ds(first_row * 40 + 1, count, stride=40), :] = xr[tile : tile + count, :]
            for n in range(count):
                row = (first_row + n) * 40
                e1[row + 4 : row + 36, :] = xr[tile + 8 + 32 * n : tile + 40 + 32 * n, :]
        for n, place in enumerate(PLACES):
            e1[pl.ds(160 + place, 16, stride=40), :] = yr[n, 0:16, :]
            e1[pl.ds(920 + place, 1), :] = yr[n, 16:17, :]
            corner, m = (1, n - 3) if n > 2 else (0, n)
            e1[pl.ds(800 + place, 3, stride=40), :] = fcr[number, corner, 3 * m : 3 * m + 3, :]
            e1[pl.ds(place, 4, stride=40), :] = fcr[number, corner + 2, 4 * m : 4 * m + 4, :]
        for target, source in ((19, 22), (2, 23)):
            e1[target * 40 : (target + 1) * 40, :] += RATIO * e1[source * 40 : (source + 1) * 40, :]
        for target, source in ((35, 37), (3, 1)):
            place = pl.ds(target, 22, stride=40)
            e1[place, :] = e1[place, :] + RATIO * e1[pl.ds(source, 22, stride=40), :]
        for place in (1, 37):
            e1[pl.ds(place, 22, stride=40), :] = jnp.zeros((22, 128), F32)

        def time_level2(n):
            t2[rows(n * 176, 176), :] = times(e1[rows(n * 176, 176), :], m2)

        loop(5, time_level2, unroll=5)

        def t2_row(i):
            return t2[i * 40 : (i + 1) * 40, :]

        p_now, q_after = t2_row(0), None
        for k in range(-2, 8):
            if k == 7:
                q_after, p_after = t2_row(20), None
            else:
                m = 1 if k == -2 else 6 + 2 * k
                even, odd = t2_row(m), t2_row(m + 1)
                q_after, p_after = q_of(even, odd), p_of(even, odd)
            n = (k + 2) * 40
            a2[0, n : n + 40, :] = low_of(p_now, q_after)
            a2[1, n : n + 40, :] = high_of(p_now, q_after)
            p_now = p_after
        a2[0, 400:440, :] = t2_row(3)
        a2[0, 440:480, :] = t2_row(21)

        def y_level2_of(xb, k):
            e = [a2[xb, pl.ds(k * 40 + j, 18, stride=2), :] for j in range(4)]
            return p_of(e[0], e[1]), q_of(e[2], e[3])

        def y_level2(k):
            place = rows(k * 24, 18)
            for xb in range(2):
                p, q = y_level2_of(xb, k)
                for yb in range(2):
                    value = high_of(p, q) if yb else low_of(p, q)
                    b = 2 * xb + yb
                    if b == 0:
                        e2[pl.ds(k * 24 + 2, 18), :] = value
                    c2[b, place, :] = shrink(old(c2, b, place, slice(None)) + value)

        def y_level2_low(k):
            e2[pl.ds(k * 24 + 2, 18), :] = low_of(*y_level2_of(0, k))

        for k in range(10, 12):
            y_level2_low(k)
        loop(10, y_level2, unroll=10)
        for source, target in ((38, 0), (39, 20)):
            e2[pl.ds(target, 12, stride=24), :] = a2[0, pl.ds(source, 12, stride=40), :]

        t3[...] = times(e2[...], m3)

        def t3_row(i):
            return t3[i * 24 : (i + 1) * 24, :]

        p_now = t3_row(10)
        for k in range(-2, 4):
            if k == 3:
                q_after, p_after = t3_row(11), None
            else:
                even, odd = t3_row(2 * k + 4), t3_row(2 * k + 5)
                q_after, p_after = q_of(even, odd), p_of(even, odd)
            n = (k + 2) * 24
            a3[0, n : n + 24, :] = low_of(p_now, q_after)
            a3[1, n : n + 24, :] = high_of(p_now, q_after)
            p_now = p_after

        lane = lax.broadcasted_iota(jnp.int32, (10, 128), 1)

        def y_level3(k):
            place = rows(k * 16, 10)
            for xb in range(2):
                e = [a3[xb, pl.ds(k * 24 + j, 10, stride=2), :] for j in range(4)]
                p, q = p_of(e[0], e[1]), q_of(e[2], e[3])
                for yb in range(2):
                    value = high_of(p, q) if yb else low_of(p, q)
                    b = 2 * xb + yb
                    value = old(c3, b, place, slice(None)) + value
                    if b == 0:
                        c3[b, place, :] = jnp.where(lane < 32, value, shrink(value))
                    else:
                        c3[b, place, :] = shrink(value)

        loop(6, y_level3, unroll=6)

        def up(low_now, high_now, low_before, high_before):
            p = low_now - RATIO * high_now
            q = high_before + RATIO * low_before
            return p + ROOT_THREE * q, ROOT_THREE * p - q

        for b in range(4):
            s3[b] = times(c3[b], m3t)

        def x_up3(k):
            for yb in range(2):
                e = [s3[b, rows((k + d) * 16, 16), :] for d in (1, 0) for b in (yb, 2 + yb)]
                even, odd = up(*e)
                p3[yb, rows(2 * k * 16, 16), :] = even
                p3[yb, rows((2 * k + 1) * 16, 16), :] = odd

        loop(5, x_up3, unroll=5)

        def y_up3(r):
            e = [p3[b, pl.ds(r * 16 + d, 9), :] for d in (1, 0) for b in (0, 1)]
            even, odd = up(*e)
            d2[pl.ds(r * 24, 9, stride=2), :] = even
            d2[pl.ds(r * 24 + 1, 9, stride=2), :] = odd

        loop(10, y_up3, unroll=10)

        lanes = lax.broadcasted_iota(jnp.int32, (240, 128), 1)
        for b in range(1, 4):
            s2[b] = times(c2[b], m2t)
        s2[0] = times(jnp.where(lanes < 64, d2[...], c2[0]), m2t)

        def x_up2(k):
            for yb in range(2):
                e = [s2[b, rows((k + d) * 24, 24), :] for d in (1, 0) for b in (yb, 2 + yb)]
                even, odd = up(*e)
                p2[yb, rows(2 * k * 24, 24), :] = even
                p2[yb, rows((2 * k + 1) * 24, 24), :] = odd

        loop(9, x_up2, unroll=9)

        def y_up2(r):
            e = [p2[b, pl.ds(r * 24 + d, 17), :] for d in (1, 0) for b in (0, 1)]
            even, odd = up(*e)
            d1[pl.ds(r * 40 + 6, 17, stride=2), :] = even
            d1[pl.ds(r * 40 + 7, 17, stride=2), :] = odd

        loop(18, y_up2, unroll=6)

        wait(f0)
        for tb in range(2):
            t0[tb, pl.ds(64, 32, stride=72), :] = cr[tb, 0:32, :]
            corners = [fcr[number, n, used + tb : used + tb + 1, :] for n, (_, used) in enumerate(CORNERS)]
            starts = []
            for ref, low_row, corner in ((qr, 72, corners[0]), (pr, 176, corners[2])):
                after = ROOT_THREE * corner
                low, place, high = (ref, 31, 63) if tb else (xr, low_row + 31, 95)
                low[place : place + 1, :] = low[place : place + 1, :] + RATIO * after
                ref[high : high + 1, :] = ref[high : high + 1, :] + after
                starts.append(ref[96:97, :] if tb else xr[low_row - 70 : low_row - 69, :])
            for place, p, q, scale in (
                (pl.ds(2, 32), cr[2 + tb, 0:32, :], ROOT_THREE * f0y[tb, 0:32, :], 1.0),
                (pl.ds(0, 1), corners[3], starts[1], 1.0),
                (pl.ds(34, 1), corners[1], starts[0], 1.0 / ROOT_THREE),
            ):
                cb[tb, place, :] = scale * low_of(p, q)
                cb[2 + tb, place, :] = scale * high_of(p, q)
        level1_ends(inner, inner_last)
        level1_ends(edge, level1(edge))
        for yb in range(2):
            for tb in range(2):
                e = [cb[2 * yb + tb, pl.ds(j, 17, stride=2), :] for j in range(4)]
                p, q = p_of(e[0], e[1]), q_of(e[2], e[3])
                for xb in range(2):
                    band = 4 * xb + 2 * yb + tb
                    if band:
                        value = high_of(p, q) if xb else low_of(p, q)
                        place = pl.ds(7, 17, stride=40)
                        c1[band - 1, place, :] = shrink(old(c1, band - 1, place, slice(None)) + value)

        time_up1_pieces([(0, 40), (640, 680)] + [(row * 40 + y, row * 40 + y + 8) for row in range(1, 16) for y in (0, 32)])

        def time_up1(n):
            place = rows(n * 136, 136)
            lo = d1[rows(40 + n * 136, 136), :]
            result = times(jnp.concatenate([lo, c1[0, place, :]], axis=1), m1t)
            s1[0, 0, place, :] = result[:, :128]
            s1[1, 0, place, :] = result[:, 128:]

        loop(5, time_up1, unroll=5)

        up_parts = [(chunk, th) for chunk in range(4) for th in range(2)]

        def y_up1(row, chunk, th):
            result = []
            for xb in range(2):
                e = [
                    s1[th, 2 * xb + yb, pl.ds(row * 40 + d + 8 * chunk, 8), :]
                    for d in (8, 7) for yb in range(2)
                ]
                result.append(up(*e))
            return [(result[0][n], result[1][n]) for n in range(2)]

        def q_next(low, high):
            return high + RATIO * low

        def up1(first_k, i, qs):
            k = first_k + i
            after = []
            n = 0
            for chunk, th in up_parts:
                for parity, (low, high) in enumerate(y_up1(k + 1, chunk, th)):
                    p = low - RATIO * high
                    start = k * 128 + 16 * chunk + parity
                    reb[th, pl.ds(start, 8, stride=2), :] = p + ROOT_THREE * qs[n]
                    reb[th, pl.ds(start + 64, 8, stride=2), :] = ROOT_THREE * p - qs[n]
                    after.append(q_next(low, high))
                    n += 1
            return tuple(after)

        def synthesis_half(first_k):
            start = tuple(q_next(*one) for chunk, th in up_parts for one in y_up1(first_k, chunk, th))
            lax.fori_loop(0, 8, functools.partial(up1, first_k), start, unroll=2)

        return synthesis_half

    synthesis = iteration(1, iteration(0, None))
    synthesis(0)
    synthesis(8)

    def finish(r):
        for th in range(2):
            out[r, :, th * 128 : (th + 1) * 128] = reb[th, rows(r * 64, 64), :]

    loop(32, finish, unroll=2)


def solution(mesh):
    nx, ny = mesh.shape["gx"], mesh.shape["gy"]

    def v(*shape):
        return pltpu.VMEM(shape, F32)

    def b(*shape):
        return pltpu.VMEM(shape, BF16)

    scratch = [
        pltpu.VMEM((32, 64, 256), jnp.int32),
        b(768, 256), b(768, 256), b(384, 128), b(384, 128), b(384, 128), b(384, 128),
        v(2, 32 * 72, 128), v(7, 17 * 40, 128), v(24 * 40, 128),
        v(22 * 40, 128), v(2, 12 * 40, 128), v(4, 10 * 24, 128), v(12 * 24, 128),
        v(12 * 24, 128), v(2, 6 * 24, 128), v(4, 6 * 16, 128),
        v(4, 6 * 16, 128), v(2, 10 * 16, 128), v(10 * 24, 128),
        v(4, 10 * 24, 128), v(2, 18 * 24, 128), v(18 * 40, 128),
        v(2, 4, 17 * 40, 128), v(2, 32 * 64, 128), v(4, 40, 128),
        v(2, 72, 128), v(2, 72, 128), v(104, 128), v(104, 128), v(4, 40, 128), v(2, 104, 128), v(2, 104, 128), v(2, 4, 40, 128),
        v(240, 128), v(7, 24, 128), v(2, 240, 128), v(2, 7, 24, 128), v(4, 24, 128), v(2, 4, 24, 128),
        pltpu.SemaphoreType.DMA((1,)), pltpu.SemaphoreType.DMA((24,)), pltpu.SemaphoreType.DMA((24,)),
    ]

    def on_device(counts):
        return pl.pallas_call(
            functools.partial(kernel, nx, ny),
            out_shape=jax.ShapeDtypeStruct(counts.shape, F32),
            in_specs=[pl.BlockSpec(memory_space=pltpu.HBM)],
            out_specs=pl.BlockSpec(memory_space=pltpu.VMEM),
            scratch_shapes=scratch,
            compiler_params=pltpu.CompilerParams(
                collective_id=0, has_side_effects=True, vmem_limit_bytes=50 * 1024 * 1024
            ),
        )(counts)

    spec = P(("grp", "gx"), "gy", None)
    return jax.shard_map(on_device, mesh=mesh, in_specs=(spec,), out_specs=spec, check_vma=False)
```

```python
import functools
import math

import jax
import jax.numpy as jnp
from jax import lax
from jax.experimental import pallas as pl
from jax.experimental.pallas import tpu as pltpu
from jax.sharding import PartitionSpec as P

ROOT_THREE = math.sqrt(3.0)
TAP_SCALE = 4.0 * math.sqrt(2.0)
H = [
    (1.0 + ROOT_THREE) / TAP_SCALE,
    (3.0 + ROOT_THREE) / TAP_SCALE,
    (3.0 - ROOT_THREE) / TAP_SCALE,
    (1.0 - ROOT_THREE) / TAP_SCALE,
]
G = [H[3], -H[2], H[1], -H[0]]
RATIO = 2.0 - ROOT_THREE
SPATIAL_SCALE = H[0] * H[0]
THRESHOLD = 0.1
MESH = pl.DeviceIdType.MESH
F32 = jnp.float32
BF16 = jnp.bfloat16

PLACES = [36, 39, 37, 0, 2, 3, 38]
CORNERS = [((-1, -1), 9), ((-1, 1), 12), ((1, -1), 12), ((1, 1), 16)]


def shrink(values):
    return values - jnp.clip(values, -THRESHOLD, THRESHOLD)


def p_of(even, odd):
    return even + ROOT_THREE * odd


def q_of(even, odd):
    return ROOT_THREE * even - odd


def q_even(even, odd):
    return even - (1.0 / ROOT_THREE) * odd


def low_of(p, q_after):
    return p + RATIO * q_after


def high_of(p, q_after):
    return q_after - RATIO * p


def loop(count, body, unroll=4):
    def step(i, carry):
        body(i)
        return carry

    lax.fori_loop(0, count, step, 0, unroll=unroll)


def rows(start, size):
    return pl.ds(pl.multiple_of(start, 8), size)


def build_matrix(ref, length, padded, transposed):
    t = lax.broadcasted_iota(jnp.int32, (padded, padded), 1 if transposed else 0)
    c = lax.broadcasted_iota(jnp.int32, (padded, padded), 0 if transposed else 1)
    half = c >= length // 2
    j = (t - 2 * jnp.where(half, c - length // 2, c)) & (length - 1)
    value = jnp.zeros((padded, padded), F32)
    for tap in range(4):
        tap_value = jnp.where(half, G[tap] * SPATIAL_SCALE, H[tap] * SPATIAL_SCALE)
        value = jnp.where(j == tap, tap_value, value)
    if padded > length:
        value = jnp.where((t < length) & (c < length), value, 0.0)
    high = value.astype(BF16)
    low = (value - high.astype(F32)).astype(BF16)
    ref[0:padded, :] = high
    ref[padded : 2 * padded, :] = high
    ref[2 * padded : 3 * padded, :] = low


def times(values, matrix_ref):
    high = values.astype(BF16)
    low = (values - high.astype(F32)).astype(BF16)
    left = jnp.concatenate([high, low, high], axis=1)
    return jnp.dot(left, matrix_ref[...], preferred_element_type=F32)


def functionals(entry, count, level1_q, q_last):
    def low2(i):
        return low_of(p_of(entry(i), entry(i + 1)), q_of(entry(i + 2), entry(i + 3)))

    n = count - 8
    return [
        q_last(entry(0), entry(1)),
        q_last(low2(0), low2(2)),
        level1_q,
        p_of(entry(n + 4), entry(n + 5)),
        entry(n + 6),
        entry(n + 7),
        p_of(low2(n), low2(n + 2)),
    ]


def kernel(
    nx, ny,
    counts_hbm, out, counts, weights, weighted, m1, m1t, m2, m2t, m3, m3t,
    t0, c1, e1, t2, a2, c2, e2, t3, a3, c3,
    s3, p3, d2, s2, p2, d1, s1, reb, cb,
    f0q, f0p, fq, fp, f0y, f0qr, f0pr, f0yr,
    f1x, f1y, f1xr, f1yr, fc, fcr,
    local_sem, send_sem, recv_sem,
):
    gx = lax.axis_index("gx")
    gy = lax.axis_index("gy")

    def device(dx, dy):
        where = {}
        if dx:
            where["gx"] = lax.rem(gx + dx + nx, nx)
        if dy:
            where["gy"] = lax.rem(gy + dy + ny, ny)
        return where

    load = pltpu.make_async_copy(counts_hbm, counts, local_sem.at[0])
    load.start()

    barrier = pltpu.get_barrier_semaphore()
    around = [(dx, dy) for dx in (-1, 0, 1) for dy in (-1, 0, 1) if dx or dy]
    for dx, dy in around:
        pl.semaphore_signal(barrier, inc=1, device_id=device(dx, dy), device_id_type=MESH)

    def send(first_sem, transfers):
        copies = []
        for n, (source, target, dx, dy) in enumerate(transfers):
            copy = pltpu.make_async_remote_copy(
                src_ref=source,
                dst_ref=target,
                send_sem=send_sem.at[first_sem + n],
                recv_sem=recv_sem.at[first_sem + n],
                device_id=device(dx, dy),
                device_id_type=MESH,
            )
            copy.start()
            copies.append(copy)
        return copies

    def wait(copies):
        for copy in copies:
            copy.wait()

    build_matrix(m1, 256, 256, False)
    for ref in (f0q, f0p):
        for tb in range(2):
            ref[tb, 64:72, :] = jnp.zeros((8, 128), F32)
    for n in range(4):
        f0y[n, 32:40, :] = jnp.zeros((8, 128), F32)
        for place in (1, 35):
            cb[n, place : place + 1, :] = jnp.zeros((1, 128), F32)
    for tb in range(2):
        t0[tb, pl.ds(65, 32, stride=72), :] = jnp.zeros((32, 128), F32)
    for place in (1, 21):
        e2[pl.ds(place, 12, stride=24), :] = jnp.zeros((12, 128), F32)
    e1[...] = jnp.zeros((960, 128), F32)
    f1y[...] = jnp.zeros((7, 24, 128), F32)
    load.wait()

    def iteration(number):
        first = number == 0
        sem = 12 * number

        def old(ref, *index):
            return 0.0 if first else ref[index]

        qr, pr, cr = f0qr.at[number], f0pr.at[number], f0yr.at[number]
        xr, yr = f1xr.at[number], f1yr.at[number]

        def time_rows(n):
            place = rows(n * 256, 256)
            if first:
                observed = counts[pl.ds(n * 4, 4)].reshape(256, 256).astype(F32) * (1.0 / 64.0)
                weight = 1.0 / (1.0 + jnp.abs(observed))
                values = weight * observed
                weights[place, :] = weight
                weighted[place, :] = values
            else:
                rebuilt = jnp.concatenate([reb[0, place, :], reb[1, place, :]], axis=1)
                values = weighted[place, :] - weights[place, :] * rebuilt
            result = times(values, m1)
            for i in range(4):
                for tb in range(2):
                    t0[tb, rows((n * 4 + i) * 72, 64), :] = result[
                        i * 64 : (i + 1) * 64, tb * 128 : (tb + 1) * 128
                    ]

        t0[0, pl.ds(64, 32, stride=72), :] = jnp.zeros((32, 128), F32)

        def y_low(read):
            e = [read(j) for j in range(4)]
            return low_of(p_of(e[0], e[1]), q_of(e[2], e[3]))

        def low_pair(k):
            return [
                [
                    y_low(lambda j: t0[0, pl.ds((2 * k + i) * 72 + 16 * chunk + j, 8, stride=2), :])
                    for i in range(2)
                ]
                for chunk in range(4)
            ]

        def low_store(k, chunk, value):
            e1[pl.ds((k + 4) * 40 + 4 + 8 * chunk, 8), :] = value

        def low_band(first_k, count):
            def low_step(n, ps):
                k = first_k + n
                after = low_pair(k + 1)
                for chunk in range(4):
                    low_store(k, chunk, low_of(ps[chunk], q_of(*after[chunk])))
                return tuple(p_of(*one) for one in after)

            ps = tuple(p_of(*one) for one in low_pair(first_k))
            return lax.fori_loop(0, count, low_step, ps, unroll=4)

        def y_level1_q(places):
            e1[pl.ds(161 + 40 * places, 8, stride=40), :] = ROOT_THREE * y_low(
                lambda j: f0y[0, pl.ds(2 * places + j, 8, stride=2), :]
            )

        def x_functionals(kind):
            for base, part in ((0, slice(4, 36)), (1, slice(1, 2))):

                def entry(i):
                    return e1[i * 40 + part.start : i * 40 + part.stop, :]

                values = functionals(lambda i: entry(4 + i), 16, entry(23), q_of)
                for n, value in enumerate(values[3:] if kind else values[:3]):
                    tile = 104 * kind
                    start = tile + n if base else tile + 8 + 32 * n
                    f1x[start : start + (1 if base else 32), :] = value

        def half(number_of_half):
            loop(4, lambda n: time_rows(n + 4 * number_of_half))
            start = 16 * number_of_half * 72
            for tb in range(2):
                column = [t0[tb, pl.ds(start + y, 16, stride=72), :] for y in (0, 1, 62, 63)]
                place = pl.ds(16 * number_of_half, 16)
                f0y[tb, place, :] = q_even(column[0], column[1])
                f0y[2 + tb, place, :] = p_of(column[2], column[3])
                if number_of_half:
                    f0p[tb, 0:64, :] = p_of(t0[tb, 2160:2224, :], t0[tb, 2232:2296, :])
                else:
                    f0q[tb, 0:64, :] = q_of(t0[tb, 0:64, :], t0[tb, 72:136, :])

        def y_functionals(source, base, size, stride, level1_q, target):
            def entry(i):
                return source[pl.ds(base + i, size, stride=stride) if size > 1 else pl.ds(base + i, 1), :]

            for n, value in enumerate(functionals(entry, 32, source[level1_q, :], q_even)):
                if target is None:
                    corner, start = 2 * (size - 3) + (n > 2), (n - 3 * (n > 2)) * size
                    fc[corner, start : start + size, :] = value
                else:
                    f1y[n, target : target + size, :] = value

        def corner_level1(n, source):
            for tb in range(2):
                place = slice(CORNERS[n][1] + tb, CORNERS[n][1] + tb + 1)
                fc[n, place, :] = q_even(source[tb, 0:1, :], source[tb, 1:2, :])
                place = slice(CORNERS[n + 1][1] + tb, CORNERS[n + 1][1] + tb + 1)
                fc[n + 1, place, :] = p_of(source[tb, 62:63, :], source[tb, 63:64, :])

        def corner_transfers(start):
            return [
                (fc.at[n, 0 : used + 2], fcr.at[number, n, 0 : used + 2], dx, dy)
                for n, ((dx, dy), used) in enumerate(CORNERS)
            ][start : start + 2]

        half(1)
        ps = low_band(8, 7)
        for chunk in range(4):
            low_store(15, chunk, ps[chunk])
        y_level1_q(8)
        x_functionals(1)
        y_functionals(f1x, 112, 4, 32, pl.ds(104, 4), None)
        corner_level1(2, f0p)
        after_transfers = corner_transfers(2) + [(f1x.at[104:240], xr.at[104:240], 1, 0)]
        f1 = [] if first else send(sem + 4, after_transfers)

        half(0)
        low_band(0, 8)
        for chunk in range(4):
            low_store(19, chunk, y_low(lambda j: f0q[0, pl.ds(16 * chunk + j, 8, stride=2), :]))
        y_level1_q(0)
        e1[921:922, :] = q_of(f0q[0, 0:1, :], f0q[0, 1:2, :])
        x_functionals(0)
        y_functionals(f1x, 8, 3, 32, pl.ds(0, 3), None)
        corner_level1(0, f0q)
        if first:
            pl.semaphore_wait(barrier, 8)
            f1 = send(sem + 4, after_transfers)
        f1 = f1 + send(sem + 7, corner_transfers(0) + [(f1x.at[0:104], xr.at[0:104], -1, 0)])
        y_functionals(e1, 164, 16, 40, pl.ds(161, 16, stride=40), 0)
        y_functionals(e1, 924, 1, 1, pl.ds(921, 1), 16)
        f1 = f1 + send(sem + 10, [
            (f1y.at[0:3], yr.at[0:3], 0, -1),
            (f1y.at[3:7], yr.at[3:7], 0, 1),
        ])
        f0_columns = send(sem + 2, [(f0y.at[0:2], cr.at[0:2], 0, -1), (f0y.at[2:4], cr.at[2:4], 0, 1)])

        def y_level1(read):
            e = [read(j) for j in range(4)]
            p, q = p_of(e[0], e[1]), q_of(e[2], e[3])
            return [low_of(p, q), high_of(p, q)]

        def y_halo(ref, chunk, tb):
            return y_level1(lambda j: ref[tb, pl.ds(16 * chunk + j, 8, stride=2), :])

        for source, target in ((f0q, fq), (f0p, fp)):
            for chunk in range(4):
                for n, value in enumerate(y_halo(source, chunk, 1) + y_halo(source, chunk, 0)[1:]):
                    target[32 * n + 8 * chunk : 32 * n + 8 * chunk + 8, :] = value
            target[96:97, :] = q_of(source[1, 0:1, :], source[1, 1:2, :])
        f0 = send(sem, [
            (fq.at[0:97], qr.at[0:97], -1, 0),
            (fp.at[0:97], pr.at[0:97], 1, 0),
        ])

        if first:
            build_matrix(m1t, 256, 256, True)
            build_matrix(m2, 128, 128, False)
            build_matrix(m2t, 128, 128, True)
            build_matrix(m3, 64, 128, False)
            build_matrix(m3t, 64, 128, True)

        def y_own(row, chunk, tb):
            return y_level1(lambda j: t0[tb, pl.ds(row * 72 + 16 * chunk + j, 8, stride=2), :])

        def level1_store(k, chunk, tb, yb, p, q):
            for xb in range(2):
                band = 4 * xb + 2 * yb + tb
                if band:
                    value = high_of(p, q) if xb else low_of(p, q)
                    place = rows((k + 1) * 40 + 8 + 8 * chunk, 8)
                    c1[band - 1, place, :] = shrink(old(c1, band - 1, place, slice(None)) + value)

        def pair(k, parts):
            result = []
            for chunk, tb in parts:
                first_row, second_row = y_own(2 * k, chunk, tb), y_own(2 * k + 1, chunk, tb)
                result += [(first_row[yb], second_row[yb]) for yb in range(2)]
            return result

        def store_all(k, parts, ps, qs):
            for n, (chunk, tb) in enumerate(parts):
                for yb in range(2):
                    level1_store(k, chunk, tb, yb, ps[2 * n + yb], qs[2 * n + yb])

        def level1(parts):
            def step(k, ps):
                after = pair(k + 1, parts)
                store_all(k, parts, ps, [q_of(*one) for one in after])
                return tuple(p_of(*one) for one in after)

            return lax.fori_loop(0, 15, step, tuple(p_of(*one) for one in pair(0, parts)), unroll=3)

        def received(ref, low_row, chunk, tb):
            if tb:
                return [ref[32 * yb + 8 * chunk : 32 * yb + 8 * chunk + 8, :] for yb in range(2)]
            place = low_row + 8 * chunk
            return [xr[place : place + 8, :], ref[64 + 8 * chunk : 72 + 8 * chunk, :]]

        def level1_ends(parts, last):
            before = [value for part in parts for value in received(pr, 176, *part)]
            store_all(-1, parts, before, [q_of(*one) for one in pair(0, parts)])
            store_all(15, parts, last, [value for part in parts for value in received(qr, 72, *part)])

        inner = [(chunk, tb) for chunk in range(3) for tb in range(2)]
        edge = [(3, tb) for tb in range(2)]
        inner_last = level1(inner)

        wait(f0_columns)
        for tb in range(2):
            t0[tb, pl.ds(64, 32, stride=72), :] = cr[tb, 0:32, :]
            p, q = cr[2 + tb, 0:32, :], ROOT_THREE * f0y[tb, 0:32, :]
            cb[tb, 2:34, :] = low_of(p, q)
            cb[2 + tb, 2:34, :] = high_of(p, q)
        edge_last = level1(edge)

        def column_before(source, target):
            for yb in range(2):
                for tb in range(2):
                    e = [cb[2 * yb + tb, source(j), :] for j in range(4)]
                    p, q = p_of(e[0], e[1]), q_of(e[2], e[3])
                    for xb in range(2):
                        band = 4 * xb + 2 * yb + tb
                        if band:
                            value = high_of(p, q) if xb else low_of(p, q)
                            c1[band - 1, target, :] = shrink(old(c1, band - 1, target, slice(None)) + value)

        column_before(lambda j: pl.ds(2 + j, 15, stride=2), pl.ds(47, 15, stride=40))

        def time_up1(b, pieces):
            def band(tb):
                if b == 0 and tb == 0:
                    return [d1[40 + start : 40 + stop, :] for start, stop in pieces]
                return [c1[2 * b - 1 + tb, start:stop, :] for start, stop in pieces]

            values = jnp.concatenate([jnp.concatenate(band(tb), axis=0) for tb in range(2)], axis=1)
            result = times(values, m1t)
            n = 0
            for start, stop in pieces:
                for th in range(2):
                    s1[th, b, start:stop, :] = result[n : n + stop - start, th * 128 : (th + 1) * 128]
                n += stop - start

        inner_rows = [(40, 240), (240, 440), (440, 640)]
        end_rows = [(0, 40), (640, 680)]
        for piece in inner_rows:
            for b in range(1, 4):
                time_up1(b, [piece])
        wait(f1)

        for tile, first_row, count in ((0, 20, 3), (104, 0, 4)):
            e1[pl.ds(first_row * 40 + 1, count, stride=40), :] = xr[tile : tile + count, :]
            for n in range(count):
                row = (first_row + n) * 40
                e1[row + 4 : row + 36, :] = xr[tile + 8 + 32 * n : tile + 40 + 32 * n, :]
        for n, place in enumerate(PLACES):
            e1[pl.ds(160 + place, 16, stride=40), :] = yr[n, 0:16, :]
            e1[pl.ds(920 + place, 1), :] = yr[n, 16:17, :]
            corner, m = (1, n - 3) if n > 2 else (0, n)
            e1[pl.ds(800 + place, 3, stride=40), :] = fcr[number, corner, 3 * m : 3 * m + 3, :]
            e1[pl.ds(place, 4, stride=40), :] = fcr[number, corner + 2, 4 * m : 4 * m + 4, :]
        for target, source in ((19, 22), (2, 23)):
            e1[target * 40 : (target + 1) * 40, :] += RATIO * e1[source * 40 : (source + 1) * 40, :]
        for target, source in ((35, 37), (3, 1)):
            place = pl.ds(target, 22, stride=40)
            e1[place, :] = e1[place, :] + RATIO * e1[pl.ds(source, 22, stride=40), :]
        for place in (1, 37):
            e1[pl.ds(place, 22, stride=40), :] = jnp.zeros((22, 128), F32)

        def time_level2(n):
            t2[rows(n * 176, 176), :] = times(e1[rows(n * 176, 176), :], m2)

        loop(5, time_level2, unroll=5)

        def t2_row(i):
            return t2[i * 40 : (i + 1) * 40, :]

        p_now, q_after = t2_row(0), None
        for k in range(-2, 8):
            if k == 7:
                q_after, p_after = t2_row(20), None
            else:
                m = 1 if k == -2 else 6 + 2 * k
                even, odd = t2_row(m), t2_row(m + 1)
                q_after, p_after = q_of(even, odd), p_of(even, odd)
            n = (k + 2) * 40
            a2[0, n : n + 40, :] = low_of(p_now, q_after)
            a2[1, n : n + 40, :] = high_of(p_now, q_after)
            p_now = p_after
        a2[0, 400:440, :] = t2_row(3)
        a2[0, 440:480, :] = t2_row(21)

        def y_level2_of(xb, k):
            e = [a2[xb, pl.ds(k * 40 + j, 18, stride=2), :] for j in range(4)]
            return p_of(e[0], e[1]), q_of(e[2], e[3])

        def y_level2(k):
            place = rows(k * 24, 18)
            for xb in range(2):
                p, q = y_level2_of(xb, k)
                for yb in range(2):
                    value = high_of(p, q) if yb else low_of(p, q)
                    b = 2 * xb + yb
                    if b == 0:
                        e2[pl.ds(k * 24 + 2, 18), :] = value
                    c2[b, place, :] = shrink(old(c2, b, place, slice(None)) + value)

        def y_level2_low(k):
            e2[pl.ds(k * 24 + 2, 18), :] = low_of(*y_level2_of(0, k))

        for k in range(10, 12):
            y_level2_low(k)
        loop(10, y_level2, unroll=10)
        for source, target in ((38, 0), (39, 20)):
            e2[pl.ds(target, 12, stride=24), :] = a2[0, pl.ds(source, 12, stride=40), :]

        t3[...] = times(e2[...], m3)

        def t3_row(i):
            return t3[i * 24 : (i + 1) * 24, :]

        p_now = t3_row(10)
        for k in range(-2, 4):
            if k == 3:
                q_after, p_after = t3_row(11), None
            else:
                even, odd = t3_row(2 * k + 4), t3_row(2 * k + 5)
                q_after, p_after = q_of(even, odd), p_of(even, odd)
            n = (k + 2) * 24
            a3[0, n : n + 24, :] = low_of(p_now, q_after)
            a3[1, n : n + 24, :] = high_of(p_now, q_after)
            p_now = p_after

        lane = lax.broadcasted_iota(jnp.int32, (10, 128), 1)

        def y_level3(k):
            place = rows(k * 16, 10)
            for xb in range(2):
                e = [a3[xb, pl.ds(k * 24 + j, 10, stride=2), :] for j in range(4)]
                p, q = p_of(e[0], e[1]), q_of(e[2], e[3])
                for yb in range(2):
                    value = high_of(p, q) if yb else low_of(p, q)
                    b = 2 * xb + yb
                    value = old(c3, b, place, slice(None)) + value
                    if b == 0:
                        c3[b, place, :] = jnp.where(lane < 32, value, shrink(value))
                    else:
                        c3[b, place, :] = shrink(value)

        loop(6, y_level3, unroll=6)

        def up(low_now, high_now, low_before, high_before):
            p = low_now - RATIO * high_now
            q = high_before + RATIO * low_before
            return p + ROOT_THREE * q, ROOT_THREE * p - q

        for b in range(4):
            s3[b] = times(c3[b], m3t)

        def x_up3(k):
            for yb in range(2):
                e = [s3[b, rows((k + d) * 16, 16), :] for d in (1, 0) for b in (yb, 2 + yb)]
                even, odd = up(*e)
                p3[yb, rows(2 * k * 16, 16), :] = even
                p3[yb, rows((2 * k + 1) * 16, 16), :] = odd

        loop(5, x_up3, unroll=5)

        def y_up3(r):
            e = [p3[b, pl.ds(r * 16 + d, 9), :] for d in (1, 0) for b in (0, 1)]
            even, odd = up(*e)
            d2[pl.ds(r * 24, 9, stride=2), :] = even
            d2[pl.ds(r * 24 + 1, 9, stride=2), :] = odd

        loop(10, y_up3, unroll=10)

        lanes = lax.broadcasted_iota(jnp.int32, (240, 128), 1)
        for b in range(1, 4):
            s2[b] = times(c2[b], m2t)
        s2[0] = times(jnp.where(lanes < 64, d2[...], c2[0]), m2t)

        def x_up2(k):
            for yb in range(2):
                e = [s2[b, rows((k + d) * 24, 24), :] for d in (1, 0) for b in (yb, 2 + yb)]
                even, odd = up(*e)
                p2[yb, rows(2 * k * 24, 24), :] = even
                p2[yb, rows((2 * k + 1) * 24, 24), :] = odd

        loop(9, x_up2, unroll=9)

        def y_up2(r):
            e = [p2[b, pl.ds(r * 24 + d, 17), :] for d in (1, 0) for b in (0, 1)]
            even, odd = up(*e)
            d1[pl.ds(r * 40 + 6, 17, stride=2), :] = even
            d1[pl.ds(r * 40 + 7, 17, stride=2), :] = odd

        loop(18, y_up2, unroll=6)

        for piece in inner_rows:
            time_up1(0, [piece])

        up_parts = [(chunk, th) for chunk in range(4) for th in range(2)]

        def y_up1(row, chunk, th):
            result = []
            for xb in range(2):
                e = [
                    s1[th, 2 * xb + yb, pl.ds(row * 40 + d + 8 * chunk, 8), :]
                    for d in (8, 7) for yb in range(2)
                ]
                result.append(up(*e))
            return [(result[0][n], result[1][n]) for n in range(2)]

        def q_next(low, high):
            return high + RATIO * low

        def up1(first_k, i, qs):
            k = first_k + i
            after = []
            n = 0
            for chunk, th in up_parts:
                for parity, (low, high) in enumerate(y_up1(k + 1, chunk, th)):
                    p = low - RATIO * high
                    start = k * 128 + 16 * chunk + parity
                    reb[th, pl.ds(start, 8, stride=2), :] = p + ROOT_THREE * qs[n]
                    reb[th, pl.ds(start + 64, 8, stride=2), :] = ROOT_THREE * p - qs[n]
                    after.append(q_next(low, high))
                    n += 1
            return tuple(after)

        def q_start(row):
            return tuple(q_next(*one) for chunk, th in up_parts for one in y_up1(row, chunk, th))

        lax.fori_loop(0, 14, functools.partial(up1, 1), q_start(1), unroll=2)
        if not first:
            loop(28, lambda n: finish(n + 2))

        wait(f0)
        for tb in range(2):
            corners = [fcr[number, n, used + tb : used + tb + 1, :] for n, (_, used) in enumerate(CORNERS)]
            starts = []
            for ref, low_row, corner in ((qr, 72, corners[0]), (pr, 176, corners[2])):
                after = ROOT_THREE * corner
                low, place, high = (ref, 31, 63) if tb else (xr, low_row + 31, 95)
                low[place : place + 1, :] = low[place : place + 1, :] + RATIO * after
                ref[high : high + 1, :] = ref[high : high + 1, :] + after
                starts.append(ref[96:97, :] if tb else xr[low_row - 70 : low_row - 69, :])
            for place, p, q, scale in (
                (pl.ds(0, 1), corners[3], starts[1], 1.0),
                (pl.ds(34, 1), corners[1], starts[0], 1.0 / ROOT_THREE),
            ):
                cb[tb, place, :] = scale * low_of(p, q)
                cb[2 + tb, place, :] = scale * high_of(p, q)
        level1_ends(inner, inner_last)
        level1_ends(edge, edge_last)
        column_before(lambda j: pl.ds(j, 2, stride=32), pl.ds(7, 2, stride=640))
        for b in range(4):
            time_up1(b, end_rows)
        up1(0, 0, q_start(0))
        up1(15, 0, q_start(15))

    def finish(r):
        for th in range(2):
            out[r, :, th * 128 : (th + 1) * 128] = reb[th, rows(r * 64, 64), :]

    iteration(0)
    iteration(1)
    for r in (0, 1, 30, 31):
        finish(r)


def solution(mesh):
    nx, ny = mesh.shape["gx"], mesh.shape["gy"]

    def v(*shape):
        return pltpu.VMEM(shape, F32)

    def b(*shape):
        return pltpu.VMEM(shape, BF16)

    scratch = [
        pltpu.VMEM((32, 64, 256), jnp.int32), v(2048, 256), v(2048, 256),
        b(768, 256), b(768, 256), b(384, 128), b(384, 128), b(384, 128), b(384, 128),
        v(2, 32 * 72, 128), v(7, 17 * 40, 128), v(24 * 40, 128),
        v(22 * 40, 128), v(2, 12 * 40, 128), v(4, 10 * 24, 128), v(12 * 24, 128),
        v(12 * 24, 128), v(2, 6 * 24, 128), v(4, 6 * 16, 128),
        v(4, 6 * 16, 128), v(2, 10 * 16, 128), v(10 * 24, 128),
        v(4, 10 * 24, 128), v(2, 18 * 24, 128), v(18 * 40, 128),
        v(2, 4, 17 * 40, 128), v(2, 32 * 64, 128), v(4, 40, 128),
        v(2, 72, 128), v(2, 72, 128), v(104, 128), v(104, 128), v(4, 40, 128), v(2, 104, 128), v(2, 104, 128), v(2, 4, 40, 128),
        v(240, 128), v(7, 24, 128), v(2, 240, 128), v(2, 7, 24, 128), v(4, 24, 128), v(2, 4, 24, 128),
        pltpu.SemaphoreType.DMA((1,)), pltpu.SemaphoreType.DMA((24,)), pltpu.SemaphoreType.DMA((24,)),
    ]

    def on_device(counts):
        return pl.pallas_call(
            functools.partial(kernel, nx, ny),
            out_shape=jax.ShapeDtypeStruct(counts.shape, F32),
            in_specs=[pl.BlockSpec(memory_space=pltpu.HBM)],
            out_specs=pl.BlockSpec(memory_space=pltpu.VMEM),
            scratch_shapes=scratch,
            compiler_params=pltpu.CompilerParams(
                collective_id=0, has_side_effects=True, vmem_limit_bytes=50 * 1024 * 1024
            ),
        )(counts)

    spec = P(("grp", "gx"), "gy", None)
    return jax.shard_map(on_device, mesh=mesh, in_specs=(spec,), out_specs=spec, check_vma=False)
```

```python
import functools
import math

import jax
import jax.numpy as jnp
from jax import lax
from jax.experimental import pallas as pl
from jax.experimental.pallas import tpu as pltpu
from jax.sharding import PartitionSpec as P

ROOT_THREE = math.sqrt(3.0)
TAP_SCALE = 4.0 * math.sqrt(2.0)
H = [
    (1.0 + ROOT_THREE) / TAP_SCALE,
    (3.0 + ROOT_THREE) / TAP_SCALE,
    (3.0 - ROOT_THREE) / TAP_SCALE,
    (1.0 - ROOT_THREE) / TAP_SCALE,
]
G = [H[3], -H[2], H[1], -H[0]]
RATIO = 2.0 - ROOT_THREE
SPATIAL_SCALE = H[0] * H[0]
THRESHOLD = 0.1
MESH = pl.DeviceIdType.MESH
F32 = jnp.float32
BF16 = jnp.bfloat16

PLACES = [36, 39, 37, 0, 2, 3, 38]
CORNERS = [((-1, -1), 9), ((-1, 1), 12), ((1, -1), 12), ((1, 1), 16)]


def shrink(values):
    return values - jnp.clip(values, -THRESHOLD, THRESHOLD)


def p_of(even, odd):
    return even + ROOT_THREE * odd


def q_of(even, odd):
    return ROOT_THREE * even - odd


def q_even(even, odd):
    return even - (1.0 / ROOT_THREE) * odd


def low_of(p, q_after):
    return p + RATIO * q_after


def high_of(p, q_after):
    return q_after - RATIO * p


def loop(count, body, unroll=4):
    def step(i, carry):
        body(i)
        return carry

    lax.fori_loop(0, count, step, 0, unroll=unroll)


def rows(start, size):
    return pl.ds(pl.multiple_of(start, 8), size)


def build_matrix(ref, length, padded, transposed):
    t = lax.broadcasted_iota(jnp.int32, (padded, padded), 1 if transposed else 0)
    c = lax.broadcasted_iota(jnp.int32, (padded, padded), 0 if transposed else 1)
    half = c >= length // 2
    j = (t - 2 * jnp.where(half, c - length // 2, c)) & (length - 1)
    value = jnp.zeros((padded, padded), F32)
    for tap in range(4):
        tap_value = jnp.where(half, G[tap] * SPATIAL_SCALE, H[tap] * SPATIAL_SCALE)
        value = jnp.where(j == tap, tap_value, value)
    if padded > length:
        value = jnp.where((t < length) & (c < length), value, 0.0)
    high = value.astype(BF16)
    low = (value - high.astype(F32)).astype(BF16)
    ref[0:padded, :] = high
    ref[padded : 2 * padded, :] = high
    ref[2 * padded : 3 * padded, :] = low


def times(values, matrix_ref):
    high = values.astype(BF16)
    low = (values - high.astype(F32)).astype(BF16)
    left = jnp.concatenate([high, low, high], axis=1)
    return jnp.dot(left, matrix_ref[...], preferred_element_type=F32)


def functionals(entry, count, level1_q, q_last):
    def low2(i):
        return low_of(p_of(entry(i), entry(i + 1)), q_of(entry(i + 2), entry(i + 3)))

    n = count - 8
    return [
        q_last(entry(0), entry(1)),
        q_last(low2(0), low2(2)),
        level1_q,
        p_of(entry(n + 4), entry(n + 5)),
        entry(n + 6),
        entry(n + 7),
        p_of(low2(n), low2(n + 2)),
    ]


def kernel(
    nx, ny,
    counts_hbm, out, counts, weights, weighted, m1, m1t, m2, m2t, m3, m3t,
    t0, c1, e1, t2, a2, c2, e2, t3, a3, c3,
    s3, p3, d2, s2, p2, d1, s1, reb, cb,
    f0q, f0p, fq, fp, f0y, f0qr, f0pr, f0yr,
    f1x, f1y, f1xr, f1yr, fc, fcr,
    local_sem, send_sem, recv_sem,
):
    gx = lax.axis_index("gx")
    gy = lax.axis_index("gy")

    def device(dx, dy):
        where = {}
        if dx:
            where["gx"] = lax.rem(gx + dx + nx, nx)
        if dy:
            where["gy"] = lax.rem(gy + dy + ny, ny)
        return where

    load = pltpu.make_async_copy(counts_hbm, counts, local_sem.at[0])
    load.start()

    barrier = pltpu.get_barrier_semaphore()
    around = [(dx, dy) for dx in (-1, 0, 1) for dy in (-1, 0, 1) if dx or dy]
    for dx, dy in around:
        pl.semaphore_signal(barrier, inc=1, device_id=device(dx, dy), device_id_type=MESH)

    def send(first_sem, transfers, start=True):
        copies = []
        for n, (source, target, dx, dy) in enumerate(transfers):
            copy = pltpu.make_async_remote_copy(
                src_ref=source,
                dst_ref=target,
                send_sem=send_sem.at[first_sem + n],
                recv_sem=recv_sem.at[first_sem + n],
                device_id=device(dx, dy),
                device_id_type=MESH,
            )
            if start:
                copy.start()
            copies.append(copy)
        return copies

    def wait(copies):
        for copy in copies:
            copy.wait()

    build_matrix(m1, 256, 256, False)
    for ref in (f0q, f0p):
        for tb in range(2):
            ref[tb, 64:72, :] = jnp.zeros((8, 128), F32)
    for n in range(4):
        f0y[n, 32:40, :] = jnp.zeros((8, 128), F32)
        for place in (1, 35):
            cb[n, place : place + 1, :] = jnp.zeros((1, 128), F32)
    for tb in range(2):
        t0[tb, pl.ds(65, 32, stride=72), :] = jnp.zeros((32, 128), F32)
    for place in (1, 21):
        e2[pl.ds(place, 12, stride=24), :] = jnp.zeros((12, 128), F32)
    e1[...] = jnp.zeros((960, 128), F32)
    f1y[...] = jnp.zeros((7, 24, 128), F32)
    load.wait()

    def iteration(number):
        first = number == 0
        sem = 12 * number

        def old(ref, *index):
            return 0.0 if first else ref[index]

        qr, pr, cr = f0qr.at[number], f0pr.at[number], f0yr.at[number]
        xr, yr = f1xr.at[number], f1yr.at[number]

        def time_rows(n):
            place = rows(n * 256, 256)
            if first:
                observed = counts[pl.ds(n * 4, 4)].reshape(256, 256).astype(F32) * (1.0 / 64.0)
                weight = 1.0 / (1.0 + jnp.abs(observed))
                values = weight * observed
                weights[place, :] = weight
                weighted[place, :] = values
            else:
                rebuilt = jnp.concatenate([reb[0, place, :], reb[1, place, :]], axis=1)
                values = weighted[place, :] - weights[place, :] * rebuilt
            result = times(values, m1)
            for i in range(4):
                for tb in range(2):
                    t0[tb, rows((n * 4 + i) * 72, 64), :] = result[
                        i * 64 : (i + 1) * 64, tb * 128 : (tb + 1) * 128
                    ]

        t0[0, pl.ds(64, 32, stride=72), :] = jnp.zeros((32, 128), F32)

        def y_low(read):
            e = [read(j) for j in range(4)]
            return low_of(p_of(e[0], e[1]), q_of(e[2], e[3]))

        def low_pair(k):
            return [
                [
                    y_low(lambda j: t0[0, pl.ds((2 * k + i) * 72 + 16 * chunk + j, 8, stride=2), :])
                    for i in range(2)
                ]
                for chunk in range(4)
            ]

        def low_store(k, chunk, value):
            e1[pl.ds((k + 4) * 40 + 4 + 8 * chunk, 8), :] = value

        def low_band(first_k, count):
            def low_step(n, ps):
                k = first_k + n
                after = low_pair(k + 1)
                for chunk in range(4):
                    low_store(k, chunk, low_of(ps[chunk], q_of(*after[chunk])))
                return tuple(p_of(*one) for one in after)

            ps = tuple(p_of(*one) for one in low_pair(first_k))
            return lax.fori_loop(0, count, low_step, ps, unroll=4)

        def y_level1_q(places):
            e1[pl.ds(161 + 40 * places, 8, stride=40), :] = ROOT_THREE * y_low(
                lambda j: f0y[0, pl.ds(2 * places + j, 8, stride=2), :]
            )

        def x_functionals(kind):
            for base, part in ((0, slice(4, 36)), (1, slice(1, 2))):

                def entry(i):
                    return e1[i * 40 + part.start : i * 40 + part.stop, :]

                values = functionals(lambda i: entry(4 + i), 16, entry(23), q_of)
                for n, value in enumerate(values[3:] if kind else values[:3]):
                    tile = 104 * kind
                    start = tile + n if base else tile + 8 + 32 * n
                    f1x[start : start + (1 if base else 32), :] = value

        def half(number_of_half):
            loop(4, lambda n: time_rows(n + 4 * number_of_half))
            start = 16 * number_of_half * 72
            for tb in range(2):
                column = [t0[tb, pl.ds(start + y, 16, stride=72), :] for y in (0, 1, 62, 63)]
                place = pl.ds(16 * number_of_half, 16)
                f0y[tb, place, :] = q_even(column[0], column[1])
                f0y[2 + tb, place, :] = p_of(column[2], column[3])
                if number_of_half:
                    f0p[tb, 0:64, :] = p_of(t0[tb, 2160:2224, :], t0[tb, 2232:2296, :])
                else:
                    f0q[tb, 0:64, :] = q_of(t0[tb, 0:64, :], t0[tb, 72:136, :])

        def y_functionals(source, base, size, stride, level1_q, target):
            def entry(i):
                return source[pl.ds(base + i, size, stride=stride) if size > 1 else pl.ds(base + i, 1), :]

            for n, value in enumerate(functionals(entry, 32, source[level1_q, :], q_even)):
                if target is None:
                    corner, start = 2 * (size - 3) + (n > 2), (n - 3 * (n > 2)) * size
                    fc[corner, start : start + size, :] = value
                else:
                    f1y[n, target : target + size, :] = value

        def corner_level1(n, source):
            for tb in range(2):
                place = slice(CORNERS[n][1] + tb, CORNERS[n][1] + tb + 1)
                fc[n, place, :] = q_even(source[tb, 0:1, :], source[tb, 1:2, :])
                place = slice(CORNERS[n + 1][1] + tb, CORNERS[n + 1][1] + tb + 1)
                fc[n + 1, place, :] = p_of(source[tb, 62:63, :], source[tb, 63:64, :])

        def corner_transfers(start):
            return [
                (fc.at[n, 0 : used + 2], fcr.at[number, n, 0 : used + 2], dx, dy)
                for n, ((dx, dy), used) in enumerate(CORNERS)
            ][start : start + 2]

        half(1)
        ps = low_band(8, 7)
        for chunk in range(4):
            low_store(15, chunk, ps[chunk])
        y_level1_q(8)
        x_functionals(1)
        y_functionals(f1x, 112, 4, 32, pl.ds(104, 4), None)
        corner_level1(2, f0p)
        after_transfers = corner_transfers(2) + [(f1x.at[104:240], xr.at[104:240], 1, 0)]
        f1 = [] if first else send(sem + 4, after_transfers)

        half(0)
        low_band(0, 8)
        for chunk in range(4):
            low_store(19, chunk, y_low(lambda j: f0q[0, pl.ds(16 * chunk + j, 8, stride=2), :]))
        y_level1_q(0)
        e1[921:922, :] = q_of(f0q[0, 0:1, :], f0q[0, 1:2, :])
        x_functionals(0)
        y_functionals(f1x, 8, 3, 32, pl.ds(0, 3), None)
        corner_level1(0, f0q)
        if first:
            pl.semaphore_wait(barrier, 8)
            f1 = send(sem + 4, after_transfers, start=False)
        f1_before = send(
            sem + 7, corner_transfers(0) + [(f1x.at[0:104], xr.at[0:104], -1, 0)], start=not first
        )
        if first:

            def start_all(copies):
                for copy in copies:
                    copy.start()

            pl.when(gx == 0)(lambda: start_all(f1_before[:2] + f1[:2] + f1_before[2:] + f1[2:]))
            pl.when(gx != 0)(lambda: start_all(f1[:2] + f1_before[:2] + f1[2:] + f1_before[2:]))
        f1 = f1 + f1_before
        y_functionals(e1, 164, 16, 40, pl.ds(161, 16, stride=40), 0)
        y_functionals(e1, 924, 1, 1, pl.ds(921, 1), 16)
        f1 = f1 + send(sem + 10, [
            (f1y.at[0:3], yr.at[0:3], 0, -1),
            (f1y.at[3:7], yr.at[3:7], 0, 1),
        ])
        f0_columns = send(sem + 2, [(f0y.at[0:2], cr.at[0:2], 0, -1), (f0y.at[2:4], cr.at[2:4], 0, 1)])

        def y_level1(read):
            e = [read(j) for j in range(4)]
            p, q = p_of(e[0], e[1]), q_of(e[2], e[3])
            return [low_of(p, q), high_of(p, q)]

        def y_halo(ref, chunk, tb):
            return y_level1(lambda j: ref[tb, pl.ds(16 * chunk + j, 8, stride=2), :])

        for source, target in ((f0q, fq), (f0p, fp)):
            for chunk in range(4):
                for n, value in enumerate(y_halo(source, chunk, 1) + y_halo(source, chunk, 0)[1:]):
                    target[32 * n + 8 * chunk : 32 * n + 8 * chunk + 8, :] = value
            target[96:97, :] = q_of(source[1, 0:1, :], source[1, 1:2, :])
        f0 = send(sem, [
            (fq.at[0:97], qr.at[0:97], -1, 0),
            (fp.at[0:97], pr.at[0:97], 1, 0),
        ])

        if first:
            build_matrix(m1t, 256, 256, True)
            build_matrix(m2, 128, 128, False)
            build_matrix(m2t, 128, 128, True)
            build_matrix(m3, 64, 128, False)
            build_matrix(m3t, 64, 128, True)

        def y_own(row, chunk, tb):
            return y_level1(lambda j: t0[tb, pl.ds(row * 72 + 16 * chunk + j, 8, stride=2), :])

        def level1_store(k, chunk, tb, yb, p, q):
            for xb in range(2):
                band = 4 * xb + 2 * yb + tb
                if band:
                    value = high_of(p, q) if xb else low_of(p, q)
                    place = rows((k + 1) * 40 + 8 + 8 * chunk, 8)
                    c1[band - 1, place, :] = shrink(old(c1, band - 1, place, slice(None)) + value)

        def pair(k, parts):
            result = []
            for chunk, tb in parts:
                first_row, second_row = y_own(2 * k, chunk, tb), y_own(2 * k + 1, chunk, tb)
                result += [(first_row[yb], second_row[yb]) for yb in range(2)]
            return result

        def store_all(k, parts, ps, qs):
            for n, (chunk, tb) in enumerate(parts):
                for yb in range(2):
                    level1_store(k, chunk, tb, yb, ps[2 * n + yb], qs[2 * n + yb])

        def level1(parts):
            def step(k, ps):
                after = pair(k + 1, parts)
                store_all(k, parts, ps, [q_of(*one) for one in after])
                return tuple(p_of(*one) for one in after)

            return lax.fori_loop(0, 15, step, tuple(p_of(*one) for one in pair(0, parts)), unroll=3)

        def received(ref, low_row, chunk, tb):
            if tb:
                return [ref[32 * yb + 8 * chunk : 32 * yb + 8 * chunk + 8, :] for yb in range(2)]
            place = low_row + 8 * chunk
            return [xr[place : place + 8, :], ref[64 + 8 * chunk : 72 + 8 * chunk, :]]

        def level1_ends(parts, last):
            before = [value for part in parts for value in received(pr, 176, *part)]
            store_all(-1, parts, before, [q_of(*one) for one in pair(0, parts)])
            store_all(15, parts, last, [value for part in parts for value in received(qr, 72, *part)])

        inner = [(chunk, tb) for chunk in range(3) for tb in range(2)]
        edge = [(3, tb) for tb in range(2)]
        inner_last = level1(inner)

        wait(f0_columns)
        for tb in range(2):
            t0[tb, pl.ds(64, 32, stride=72), :] = cr[tb, 0:32, :]
            p, q = cr[2 + tb, 0:32, :], ROOT_THREE * f0y[tb, 0:32, :]
            cb[tb, 2:34, :] = low_of(p, q)
            cb[2 + tb, 2:34, :] = high_of(p, q)
        edge_last = level1(edge)

        def column_before(source, target):
            for yb in range(2):
                for tb in range(2):
                    e = [cb[2 * yb + tb, source(j), :] for j in range(4)]
                    p, q = p_of(e[0], e[1]), q_of(e[2], e[3])
                    for xb in range(2):
                        band = 4 * xb + 2 * yb + tb
                        if band:
                            value = high_of(p, q) if xb else low_of(p, q)
                            c1[band - 1, target, :] = shrink(old(c1, band - 1, target, slice(None)) + value)

        column_before(lambda j: pl.ds(2 + j, 15, stride=2), pl.ds(47, 15, stride=40))

        def time_up1(b, pieces):
            def band(tb):
                if b == 0 and tb == 0:
                    return [d1[40 + start : 40 + stop, :] for start, stop in pieces]
                return [c1[2 * b - 1 + tb, start:stop, :] for start, stop in pieces]

            values = jnp.concatenate([jnp.concatenate(band(tb), axis=0) for tb in range(2)], axis=1)
            result = times(values, m1t)
            n = 0
            for start, stop in pieces:
                for th in range(2):
                    s1[th, b, start:stop, :] = result[n : n + stop - start, th * 128 : (th + 1) * 128]
                n += stop - start

        inner_rows = [(40, 240), (240, 440), (440, 640)]
        end_rows = [(0, 40), (640, 680)]
        for piece in inner_rows:
            for b in range(1, 4):
                time_up1(b, [piece])
        wait(f1)

        for tile, first_row, count in ((0, 20, 3), (104, 0, 4)):
            e1[pl.ds(first_row * 40 + 1, count, stride=40), :] = xr[tile : tile + count, :]
            for n in range(count):
                row = (first_row + n) * 40
                e1[row + 4 : row + 36, :] = xr[tile + 8 + 32 * n : tile + 40 + 32 * n, :]
        for n, place in enumerate(PLACES):
            e1[pl.ds(160 + place, 16, stride=40), :] = yr[n, 0:16, :]
            e1[pl.ds(920 + place, 1), :] = yr[n, 16:17, :]
            corner, m = (1, n - 3) if n > 2 else (0, n)
            e1[pl.ds(800 + place, 3, stride=40), :] = fcr[number, corner, 3 * m : 3 * m + 3, :]
            e1[pl.ds(place, 4, stride=40), :] = fcr[number, corner + 2, 4 * m : 4 * m + 4, :]
        for target, source in ((19, 22), (2, 23)):
            e1[target * 40 : (target + 1) * 40, :] += RATIO * e1[source * 40 : (source + 1) * 40, :]
        for target, source in ((35, 37), (3, 1)):
            place = pl.ds(target, 22, stride=40)
            e1[place, :] = e1[place, :] + RATIO * e1[pl.ds(source, 22, stride=40), :]
        for place in (1, 37):
            e1[pl.ds(place, 22, stride=40), :] = jnp.zeros((22, 128), F32)

        def time_level2(n):
            t2[rows(n * 176, 176), :] = times(e1[rows(n * 176, 176), :], m2)

        loop(5, time_level2, unroll=5)

        def t2_row(i):
            return t2[i * 40 : (i + 1) * 40, :]

        p_now, q_after = t2_row(0), None
        for k in range(-2, 8):
            if k == 7:
                q_after, p_after = t2_row(20), None
            else:
                m = 1 if k == -2 else 6 + 2 * k
                even, odd = t2_row(m), t2_row(m + 1)
                q_after, p_after = q_of(even, odd), p_of(even, odd)
            n = (k + 2) * 40
            a2[0, n : n + 40, :] = low_of(p_now, q_after)
            a2[1, n : n + 40, :] = high_of(p_now, q_after)
            p_now = p_after
        a2[0, 400:440, :] = t2_row(3)
        a2[0, 440:480, :] = t2_row(21)

        def y_level2_of(xb, k):
            e = [a2[xb, pl.ds(k * 40 + j, 18, stride=2), :] for j in range(4)]
            return p_of(e[0], e[1]), q_of(e[2], e[3])

        def y_level2(k):
            place = rows(k * 24, 18)
            for xb in range(2):
                p, q = y_level2_of(xb, k)
                for yb in range(2):
                    value = high_of(p, q) if yb else low_of(p, q)
                    b = 2 * xb + yb
                    if b == 0:
                        e2[pl.ds(k * 24 + 2, 18), :] = value
                    c2[b, place, :] = shrink(old(c2, b, place, slice(None)) + value)

        def y_level2_low(k):
            e2[pl.ds(k * 24 + 2, 18), :] = low_of(*y_level2_of(0, k))

        for k in range(10, 12):
            y_level2_low(k)
        loop(10, y_level2, unroll=10)
        for source, target in ((38, 0), (39, 20)):
            e2[pl.ds(target, 12, stride=24), :] = a2[0, pl.ds(source, 12, stride=40), :]

        t3[...] = times(e2[...], m3)

        def t3_row(i):
            return t3[i * 24 : (i + 1) * 24, :]

        p_now = t3_row(10)
        for k in range(-2, 4):
            if k == 3:
                q_after, p_after = t3_row(11), None
            else:
                even, odd = t3_row(2 * k + 4), t3_row(2 * k + 5)
                q_after, p_after = q_of(even, odd), p_of(even, odd)
            n = (k + 2) * 24
            a3[0, n : n + 24, :] = low_of(p_now, q_after)
            a3[1, n : n + 24, :] = high_of(p_now, q_after)
            p_now = p_after

        lane = lax.broadcasted_iota(jnp.int32, (10, 128), 1)

        def y_level3(k):
            place = rows(k * 16, 10)
            for xb in range(2):
                e = [a3[xb, pl.ds(k * 24 + j, 10, stride=2), :] for j in range(4)]
                p, q = p_of(e[0], e[1]), q_of(e[2], e[3])
                for yb in range(2):
                    value = high_of(p, q) if yb else low_of(p, q)
                    b = 2 * xb + yb
                    value = old(c3, b, place, slice(None)) + value
                    if b == 0:
                        c3[b, place, :] = jnp.where(lane < 32, value, shrink(value))
                    else:
                        c3[b, place, :] = shrink(value)

        loop(6, y_level3, unroll=6)

        def up(low_now, high_now, low_before, high_before):
            p = low_now - RATIO * high_now
            q = high_before + RATIO * low_before
            return p + ROOT_THREE * q, ROOT_THREE * p - q

        for b in range(4):
            s3[b] = times(c3[b], m3t)

        def x_up3(k):
            for yb in range(2):
                e = [s3[b, rows((k + d) * 16, 16), :] for d in (1, 0) for b in (yb, 2 + yb)]
                even, odd = up(*e)
                p3[yb, rows(2 * k * 16, 16), :] = even
                p3[yb, rows((2 * k + 1) * 16, 16), :] = odd

        loop(5, x_up3, unroll=5)

        def y_up3(r):
            e = [p3[b, pl.ds(r * 16 + d, 9), :] for d in (1, 0) for b in (0, 1)]
            even, odd = up(*e)
            d2[pl.ds(r * 24, 9, stride=2), :] = even
            d2[pl.ds(r * 24 + 1, 9, stride=2), :] = odd

        loop(10, y_up3, unroll=10)

        lanes = lax.broadcasted_iota(jnp.int32, (240, 128), 1)
        for b in range(1, 4):
            s2[b] = times(c2[b], m2t)
        s2[0] = times(jnp.where(lanes < 64, d2[...], c2[0]), m2t)

        def x_up2(k):
            for yb in range(2):
                e = [s2[b, rows((k + d) * 24, 24), :] for d in (1, 0) for b in (yb, 2 + yb)]
                even, odd = up(*e)
                p2[yb, rows(2 * k * 24, 24), :] = even
                p2[yb, rows((2 * k + 1) * 24, 24), :] = odd

        loop(9, x_up2, unroll=9)

        def y_up2(r):
            e = [p2[b, pl.ds(r * 24 + d, 17), :] for d in (1, 0) for b in (0, 1)]
            even, odd = up(*e)
            d1[pl.ds(r * 40 + 6, 17, stride=2), :] = even
            d1[pl.ds(r * 40 + 7, 17, stride=2), :] = odd

        loop(18, y_up2, unroll=6)

        for piece in inner_rows:
            time_up1(0, [piece])

        up_parts = [(chunk, th) for chunk in range(4) for th in range(2)]

        def y_up1(row, chunk, th):
            result = []
            for xb in range(2):
                e = [
                    s1[th, 2 * xb + yb, pl.ds(row * 40 + d + 8 * chunk, 8), :]
                    for d in (8, 7) for yb in range(2)
                ]
                result.append(up(*e))
            return [(result[0][n], result[1][n]) for n in range(2)]

        def q_next(low, high):
            return high + RATIO * low

        def up1(first_k, i, qs):
            k = first_k + i
            after = []
            n = 0
            for chunk, th in up_parts:
                for parity, (low, high) in enumerate(y_up1(k + 1, chunk, th)):
                    p = low - RATIO * high
                    start = k * 128 + 16 * chunk + parity
                    reb[th, pl.ds(start, 8, stride=2), :] = p + ROOT_THREE * qs[n]
                    reb[th, pl.ds(start + 64, 8, stride=2), :] = ROOT_THREE * p - qs[n]
                    after.append(q_next(low, high))
                    n += 1
            return tuple(after)

        def q_start(row):
            return tuple(q_next(*one) for chunk, th in up_parts for one in y_up1(row, chunk, th))

        lax.fori_loop(0, 14, functools.partial(up1, 1), q_start(1), unroll=2)
        if not first:
            loop(28, lambda n: finish(n + 2))

        def ends():
            wait(f0)
            for tb in range(2):
                corners = [fcr[number, n, used + tb : used + tb + 1, :] for n, (_, used) in enumerate(CORNERS)]
                starts = []
                for ref, low_row, corner in ((qr, 72, corners[0]), (pr, 176, corners[2])):
                    after = ROOT_THREE * corner
                    low, place, high = (ref, 31, 63) if tb else (xr, low_row + 31, 95)
                    low[place : place + 1, :] = low[place : place + 1, :] + RATIO * after
                    ref[high : high + 1, :] = ref[high : high + 1, :] + after
                    starts.append(ref[96:97, :] if tb else xr[low_row - 70 : low_row - 69, :])
                for place, p, q, scale in (
                    (pl.ds(0, 1), corners[3], starts[1], 1.0),
                    (pl.ds(34, 1), corners[1], starts[0], 1.0 / ROOT_THREE),
                ):
                    cb[tb, place, :] = scale * low_of(p, q)
                    cb[2 + tb, place, :] = scale * high_of(p, q)
            level1_ends(inner, inner_last)
            level1_ends(edge, edge_last)
            column_before(lambda j: pl.ds(j, 2, stride=32), pl.ds(7, 2, stride=640))
            for b in range(4):
                time_up1(b, end_rows)
            up1(0, 0, q_start(0))
            up1(15, 0, q_start(15))

        return ends

    def finish(r):
        for th in range(2):
            out[r, :, th * 128 : (th + 1) * 128] = reb[th, rows(r * 64, 64), :]

    iteration(0)()
    iteration(1)()
    for r in (0, 1, 30, 31):
        finish(r)


def solution(mesh):
    nx, ny = mesh.shape["gx"], mesh.shape["gy"]

    def v(*shape):
        return pltpu.VMEM(shape, F32)

    def b(*shape):
        return pltpu.VMEM(shape, BF16)

    scratch = [
        pltpu.VMEM((32, 64, 256), jnp.int32), v(2048, 256), v(2048, 256),
        b(768, 256), b(768, 256), b(384, 128), b(384, 128), b(384, 128), b(384, 128),
        v(2, 32 * 72, 128), v(7, 17 * 40, 128), v(24 * 40, 128),
        v(22 * 40, 128), v(2, 12 * 40, 128), v(4, 10 * 24, 128), v(12 * 24, 128),
        v(12 * 24, 128), v(2, 6 * 24, 128), v(4, 6 * 16, 128),
        v(4, 6 * 16, 128), v(2, 10 * 16, 128), v(10 * 24, 128),
        v(4, 10 * 24, 128), v(2, 18 * 24, 128), v(18 * 40, 128),
        v(2, 4, 17 * 40, 128), v(2, 32 * 64, 128), v(4, 40, 128),
        v(2, 72, 128), v(2, 72, 128), v(104, 128), v(104, 128), v(4, 40, 128), v(2, 104, 128), v(2, 104, 128), v(2, 4, 40, 128),
        v(240, 128), v(7, 24, 128), v(2, 240, 128), v(2, 7, 24, 128), v(4, 24, 128), v(2, 4, 24, 128),
        pltpu.SemaphoreType.DMA((1,)), pltpu.SemaphoreType.DMA((24,)), pltpu.SemaphoreType.DMA((24,)),
    ]

    def on_device(counts):
        return pl.pallas_call(
            functools.partial(kernel, nx, ny),
            out_shape=jax.ShapeDtypeStruct(counts.shape, F32),
            in_specs=[pl.BlockSpec(memory_space=pltpu.HBM)],
            out_specs=pl.BlockSpec(memory_space=pltpu.VMEM),
            scratch_shapes=scratch,
            compiler_params=pltpu.CompilerParams(
                collective_id=0, has_side_effects=True, vmem_limit_bytes=50 * 1024 * 1024
            ),
        )(counts)

    spec = P(("grp", "gx"), "gy", None)
    return jax.shard_map(on_device, mesh=mesh, in_specs=(spec,), out_specs=spec, check_vma=False)
```

```python
import functools
import math

import jax
import jax.numpy as jnp
from jax import lax
from jax.experimental import pallas as pl
from jax.experimental.pallas import tpu as pltpu
from jax.sharding import PartitionSpec as P

ROOT_THREE = math.sqrt(3.0)
TAP_SCALE = 4.0 * math.sqrt(2.0)
H = [
    (1.0 + ROOT_THREE) / TAP_SCALE,
    (3.0 + ROOT_THREE) / TAP_SCALE,
    (3.0 - ROOT_THREE) / TAP_SCALE,
    (1.0 - ROOT_THREE) / TAP_SCALE,
]
G = [H[3], -H[2], H[1], -H[0]]
RATIO = 2.0 - ROOT_THREE
SPATIAL_SCALE = H[0] * H[0]
THRESHOLD = 0.1
MESH = pl.DeviceIdType.MESH
F32 = jnp.float32
BF16 = jnp.bfloat16

PLACES = [36, 39, 37, 0, 2, 3, 38]
CORNERS = [((-1, -1), 9), ((-1, 1), 12), ((1, -1), 12), ((1, 1), 16)]


def shrink(values):
    return values - jnp.clip(values, -THRESHOLD, THRESHOLD)


def p_of(even, odd):
    return even + ROOT_THREE * odd


def q_of(even, odd):
    return ROOT_THREE * even - odd


def q_even(even, odd):
    return even - (1.0 / ROOT_THREE) * odd


def low_of(p, q_after):
    return p + RATIO * q_after


def high_of(p, q_after):
    return q_after - RATIO * p


def loop(count, body, unroll=4):
    def step(i, carry):
        body(i)
        return carry

    lax.fori_loop(0, count, step, 0, unroll=unroll)


def rows(start, size):
    return pl.ds(pl.multiple_of(start, 8), size)


def build_matrix(ref, length, padded, transposed):
    t = lax.broadcasted_iota(jnp.int32, (padded, padded), 1 if transposed else 0)
    c = lax.broadcasted_iota(jnp.int32, (padded, padded), 0 if transposed else 1)
    half = c >= length // 2
    j = (t - 2 * jnp.where(half, c - length // 2, c)) & (length - 1)
    value = jnp.zeros((padded, padded), F32)
    for tap in range(4):
        tap_value = jnp.where(half, G[tap] * SPATIAL_SCALE, H[tap] * SPATIAL_SCALE)
        value = jnp.where(j == tap, tap_value, value)
    if padded > length:
        value = jnp.where((t < length) & (c < length), value, 0.0)
    high = value.astype(BF16)
    low = (value - high.astype(F32)).astype(BF16)
    ref[0:padded, :] = high
    ref[padded : 2 * padded, :] = high
    ref[2 * padded : 3 * padded, :] = low


def times(values, matrix_ref):
    high = values.astype(BF16)
    low = (values - high.astype(F32)).astype(BF16)
    left = jnp.concatenate([high, low, high], axis=1)
    return jnp.dot(left, matrix_ref[...], preferred_element_type=F32)


def functionals(entry, count, level1_q, q_last):
    def low2(i):
        return low_of(p_of(entry(i), entry(i + 1)), q_of(entry(i + 2), entry(i + 3)))

    n = count - 8
    return [
        q_last(entry(0), entry(1)),
        q_last(low2(0), low2(2)),
        level1_q,
        p_of(entry(n + 4), entry(n + 5)),
        entry(n + 6),
        entry(n + 7),
        p_of(low2(n), low2(n + 2)),
    ]


def kernel(
    nx, ny,
    counts_hbm, out, counts, weights, weighted, m1, m1t, m2, m2t, m3, m3t,
    t0, c1, e1, t2, a2, c2, e2, t3, a3, c3,
    s3, p3, d2, s2, p2, d1, s1, reb, cb,
    f0q, f0p, fq, fp, f0y, f0qr, f0pr, f0yr,
    f1x, f1y, f1xr, f1yr, fc, fcr,
    local_sem, send_sem, recv_sem,
):
    gx = lax.axis_index("gx")
    gy = lax.axis_index("gy")

    def device(dx, dy):
        where = {}
        if dx:
            where["gx"] = lax.rem(gx + dx + nx, nx)
        if dy:
            where["gy"] = lax.rem(gy + dy + ny, ny)
        return where

    load = pltpu.make_async_copy(counts_hbm, counts, local_sem.at[0])
    load.start()

    barrier = pltpu.get_barrier_semaphore()
    around = [(dx, dy) for dx in (-1, 0, 1) for dy in (-1, 0, 1) if dx or dy]
    for dx, dy in around:
        pl.semaphore_signal(barrier, inc=1, device_id=device(dx, dy), device_id_type=MESH)

    def send(first_sem, transfers, start=True):
        copies = []
        for n, (source, target, dx, dy) in enumerate(transfers):
            copy = pltpu.make_async_remote_copy(
                src_ref=source,
                dst_ref=target,
                send_sem=send_sem.at[first_sem + n],
                recv_sem=recv_sem.at[first_sem + n],
                device_id=device(dx, dy),
                device_id_type=MESH,
            )
            if start:
                copy.start()
            copies.append(copy)
        return copies

    def wait(copies):
        for copy in copies:
            copy.wait()

    build_matrix(m1, 256, 256, False)
    for ref in (f0q, f0p):
        for tb in range(2):
            ref[tb, 64:72, :] = jnp.zeros((8, 128), F32)
    for n in range(4):
        f0y[n, 32:40, :] = jnp.zeros((8, 128), F32)
        for place in (1, 35):
            cb[n, place : place + 1, :] = jnp.zeros((1, 128), F32)
    for tb in range(2):
        t0[tb, pl.ds(65, 32, stride=72), :] = jnp.zeros((32, 128), F32)
    for place in (1, 21):
        e2[pl.ds(place, 12, stride=24), :] = jnp.zeros((12, 128), F32)
    e1[...] = jnp.zeros((960, 128), F32)
    f1y[...] = jnp.zeros((7, 24, 128), F32)
    load.wait()

    def iteration(number):
        first = number == 0
        sem = 12 * number

        def old(ref, *index):
            return 0.0 if first else ref[index]

        qr, pr, cr = f0qr.at[number], f0pr.at[number], f0yr.at[number]
        xr, yr = f1xr.at[number], f1yr.at[number]

        def time_rows(n):
            place = rows(n * 256, 256)
            if first:
                observed = counts[pl.ds(n * 4, 4)].reshape(256, 256).astype(F32) * (1.0 / 64.0)
                weight = 1.0 / (1.0 + jnp.abs(observed))
                values = weight * observed
                weights[place, :] = weight
                weighted[place, :] = values
            else:
                rebuilt = jnp.concatenate([reb[0, place, :], reb[1, place, :]], axis=1)
                values = weighted[place, :] - weights[place, :] * rebuilt
            result = times(values, m1)
            for i in range(4):
                for tb in range(2):
                    t0[tb, rows((n * 4 + i) * 72, 64), :] = result[
                        i * 64 : (i + 1) * 64, tb * 128 : (tb + 1) * 128
                    ]

        t0[0, pl.ds(64, 32, stride=72), :] = jnp.zeros((32, 128), F32)

        def y_low(read):
            e = [read(j) for j in range(4)]
            return low_of(p_of(e[0], e[1]), q_of(e[2], e[3]))

        def low_pair(k):
            return [
                [
                    y_low(lambda j: t0[0, pl.ds((2 * k + i) * 72 + 16 * chunk + j, 8, stride=2), :])
                    for i in range(2)
                ]
                for chunk in range(4)
            ]

        def low_store(k, chunk, value):
            e1[pl.ds((k + 4) * 40 + 4 + 8 * chunk, 8), :] = value

        def low_band(first_k, count):
            def low_step(n, ps):
                k = first_k + n
                after = low_pair(k + 1)
                for chunk in range(4):
                    low_store(k, chunk, low_of(ps[chunk], q_of(*after[chunk])))
                return tuple(p_of(*one) for one in after)

            ps = tuple(p_of(*one) for one in low_pair(first_k))
            return lax.fori_loop(0, count, low_step, ps, unroll=4)

        def y_level1_q(places):
            e1[pl.ds(161 + 40 * places, 8, stride=40), :] = ROOT_THREE * y_low(
                lambda j: f0y[0, pl.ds(2 * places + j, 8, stride=2), :]
            )

        def x_functionals(kind):
            for base, part in ((0, slice(4, 36)), (1, slice(1, 2))):

                def entry(i):
                    return e1[i * 40 + part.start : i * 40 + part.stop, :]

                values = functionals(lambda i: entry(4 + i), 16, entry(23), q_of)
                for n, value in enumerate(values[3:] if kind else values[:3]):
                    tile = 104 * kind
                    start = tile + n if base else tile + 8 + 32 * n
                    f1x[start : start + (1 if base else 32), :] = value

        def half(number_of_half):
            loop(4, lambda n: time_rows(n + 4 * number_of_half))
            start = 16 * number_of_half * 72
            for tb in range(2):
                column = [t0[tb, pl.ds(start + y, 16, stride=72), :] for y in (0, 1, 62, 63)]
                place = pl.ds(16 * number_of_half, 16)
                f0y[tb, place, :] = q_even(column[0], column[1])
                f0y[2 + tb, place, :] = p_of(column[2], column[3])
                if number_of_half:
                    f0p[tb, 0:64, :] = p_of(t0[tb, 2160:2224, :], t0[tb, 2232:2296, :])
                else:
                    f0q[tb, 0:64, :] = q_of(t0[tb, 0:64, :], t0[tb, 72:136, :])

        def y_functionals(source, base, size, stride, level1_q, target):
            def entry(i):
                return source[pl.ds(base + i, size, stride=stride) if size > 1 else pl.ds(base + i, 1), :]

            for n, value in enumerate(functionals(entry, 32, source[level1_q, :], q_even)):
                if target is None:
                    corner, start = 2 * (size - 3) + (n > 2), (n - 3 * (n > 2)) * size
                    fc[corner, start : start + size, :] = value
                else:
                    f1y[n, target : target + size, :] = value

        def corner_level1(n, source):
            for tb in range(2):
                place = slice(CORNERS[n][1] + tb, CORNERS[n][1] + tb + 1)
                fc[n, place, :] = q_even(source[tb, 0:1, :], source[tb, 1:2, :])
                place = slice(CORNERS[n + 1][1] + tb, CORNERS[n + 1][1] + tb + 1)
                fc[n + 1, place, :] = p_of(source[tb, 62:63, :], source[tb, 63:64, :])

        def corner_transfers(start):
            return [
                (fc.at[n, 0 : used + 2], fcr.at[number, n, 0 : used + 2], dx, dy)
                for n, ((dx, dy), used) in enumerate(CORNERS)
            ][start : start + 2]

        half(1)
        ps = low_band(8, 7)
        for chunk in range(4):
            low_store(15, chunk, ps[chunk])
        y_level1_q(8)
        x_functionals(1)
        y_functionals(f1x, 112, 4, 32, pl.ds(104, 4), None)
        corner_level1(2, f0p)
        after_transfers = corner_transfers(2) + [(f1x.at[104:240], xr.at[104:240], 1, 0)]
        f1 = [] if first else send(sem + 4, after_transfers)

        half(0)
        low_band(0, 8)
        for chunk in range(4):
            low_store(19, chunk, y_low(lambda j: f0q[0, pl.ds(16 * chunk + j, 8, stride=2), :]))
        y_level1_q(0)
        e1[921:922, :] = q_of(f0q[0, 0:1, :], f0q[0, 1:2, :])
        x_functionals(0)
        y_functionals(f1x, 8, 3, 32, pl.ds(0, 3), None)
        corner_level1(0, f0q)
        if first:
            pl.semaphore_wait(barrier, 8)
            f1 = send(sem + 4, after_transfers, start=False)
        f1_before = send(
            sem + 7, corner_transfers(0) + [(f1x.at[0:104], xr.at[0:104], -1, 0)], start=not first
        )
        if first:

            def start_all(copies):
                for copy in copies:
                    copy.start()

            pl.when(gx == 0)(lambda: start_all(f1_before[:2] + f1[:2] + f1_before[2:] + f1[2:]))
            pl.when(gx != 0)(lambda: start_all(f1[:2] + f1_before[:2] + f1[2:] + f1_before[2:]))
        f1 = f1 + f1_before
        y_functionals(e1, 164, 16, 40, pl.ds(161, 16, stride=40), 0)
        y_functionals(e1, 924, 1, 1, pl.ds(921, 1), 16)
        f1 = f1 + send(sem + 10, [
            (f1y.at[0:3], yr.at[0:3], 0, -1),
            (f1y.at[3:7], yr.at[3:7], 0, 1),
        ])
        f0_columns = send(sem + 2, [(f0y.at[0:2], cr.at[0:2], 0, -1), (f0y.at[2:4], cr.at[2:4], 0, 1)])

        def y_level1(read):
            e = [read(j) for j in range(4)]
            p, q = p_of(e[0], e[1]), q_of(e[2], e[3])
            return [low_of(p, q), high_of(p, q)]

        def y_halo(ref, chunk, tb):
            return y_level1(lambda j: ref[tb, pl.ds(16 * chunk + j, 8, stride=2), :])

        for source, target in ((f0q, fq), (f0p, fp)):
            for chunk in range(4):
                for n, value in enumerate(y_halo(source, chunk, 1) + y_halo(source, chunk, 0)[1:]):
                    target[32 * n + 8 * chunk : 32 * n + 8 * chunk + 8, :] = value
            target[96:97, :] = q_of(source[1, 0:1, :], source[1, 1:2, :])
        f0 = send(sem, [
            (fq.at[0:97], qr.at[0:97], -1, 0),
            (fp.at[0:97], pr.at[0:97], 1, 0),
        ])

        if first:
            build_matrix(m1t, 256, 256, True)
            build_matrix(m2, 128, 128, False)
            build_matrix(m2t, 128, 128, True)
            build_matrix(m3, 64, 128, False)
            build_matrix(m3t, 64, 128, True)

        def y_own(row, chunk, tb):
            return y_level1(lambda j: t0[tb, pl.ds(row * 72 + 16 * chunk + j, 8, stride=2), :])

        def level1_store(k, chunk, tb, yb, p, q):
            for xb in range(2):
                band = 4 * xb + 2 * yb + tb
                if band:
                    value = high_of(p, q) if xb else low_of(p, q)
                    place = rows((k + 1) * 40 + 8 + 8 * chunk, 8)
                    c1[band - 1, place, :] = shrink(old(c1, band - 1, place, slice(None)) + value)

        def pair(k, parts):
            result = []
            for chunk, tb in parts:
                first_row, second_row = y_own(2 * k, chunk, tb), y_own(2 * k + 1, chunk, tb)
                result += [(first_row[yb], second_row[yb]) for yb in range(2)]
            return result

        def store_all(k, parts, ps, qs):
            for n, (chunk, tb) in enumerate(parts):
                for yb in range(2):
                    level1_store(k, chunk, tb, yb, ps[2 * n + yb], qs[2 * n + yb])

        def level1(parts):
            def step(k, ps):
                after = pair(k + 1, parts)
                store_all(k, parts, ps, [q_of(*one) for one in after])
                return tuple(p_of(*one) for one in after)

            return lax.fori_loop(0, 15, step, tuple(p_of(*one) for one in pair(0, parts)), unroll=3)

        def received(ref, low_row, chunk, tb):
            if tb:
                return [ref[32 * yb + 8 * chunk : 32 * yb + 8 * chunk + 8, :] for yb in range(2)]
            place = low_row + 8 * chunk
            return [xr[place : place + 8, :], ref[64 + 8 * chunk : 72 + 8 * chunk, :]]

        def level1_ends(parts, last):
            before = [value for part in parts for value in received(pr, 176, *part)]
            store_all(-1, parts, before, [q_of(*one) for one in pair(0, parts)])
            store_all(15, parts, last, [value for part in parts for value in received(qr, 72, *part)])

        inner = [(chunk, tb) for chunk in range(3) for tb in range(2)]
        edge = [(3, tb) for tb in range(2)]
        inner_last = level1(inner)

        wait(f0_columns)
        for tb in range(2):
            t0[tb, pl.ds(64, 32, stride=72), :] = cr[tb, 0:32, :]
            p, q = cr[2 + tb, 0:32, :], ROOT_THREE * f0y[tb, 0:32, :]
            cb[tb, 2:34, :] = low_of(p, q)
            cb[2 + tb, 2:34, :] = high_of(p, q)
        edge_last = level1(edge)

        def column_before(source, target):
            for yb in range(2):
                for tb in range(2):
                    e = [cb[2 * yb + tb, source(j), :] for j in range(4)]
                    p, q = p_of(e[0], e[1]), q_of(e[2], e[3])
                    for xb in range(2):
                        band = 4 * xb + 2 * yb + tb
                        if band:
                            value = high_of(p, q) if xb else low_of(p, q)
                            c1[band - 1, target, :] = shrink(old(c1, band - 1, target, slice(None)) + value)

        column_before(lambda j: pl.ds(2 + j, 15, stride=2), pl.ds(47, 15, stride=40))

        def time_up1(b, pieces):
            def band(tb):
                if b == 0 and tb == 0:
                    return [d1[40 + start : 40 + stop, :] for start, stop in pieces]
                return [c1[2 * b - 1 + tb, start:stop, :] for start, stop in pieces]

            values = jnp.concatenate([jnp.concatenate(band(tb), axis=0) for tb in range(2)], axis=1)
            result = times(values, m1t)
            n = 0
            for start, stop in pieces:
                for th in range(2):
                    s1[th, b, start:stop, :] = result[n : n + stop - start, th * 128 : (th + 1) * 128]
                n += stop - start

        inner_rows = [(40, 240), (240, 440), (440, 640)]
        end_rows = [(0, 40), (640, 680)]
        for piece in inner_rows:
            for b in range(1, 4):
                time_up1(b, [piece])
        wait(f1)

        for tile, first_row, count in ((0, 20, 3), (104, 0, 4)):
            e1[pl.ds(first_row * 40 + 1, count, stride=40), :] = xr[tile : tile + count, :]
            for n in range(count):
                row = (first_row + n) * 40
                e1[row + 4 : row + 36, :] = xr[tile + 8 + 32 * n : tile + 40 + 32 * n, :]
        for n, place in enumerate(PLACES):
            e1[pl.ds(160 + place, 16, stride=40), :] = yr[n, 0:16, :]
            e1[pl.ds(920 + place, 1), :] = yr[n, 16:17, :]
            corner, m = (1, n - 3) if n > 2 else (0, n)
            e1[pl.ds(800 + place, 3, stride=40), :] = fcr[number, corner, 3 * m : 3 * m + 3, :]
            e1[pl.ds(place, 4, stride=40), :] = fcr[number, corner + 2, 4 * m : 4 * m + 4, :]
        for target, source in ((19, 22), (2, 23)):
            e1[target * 40 : (target + 1) * 40, :] += RATIO * e1[source * 40 : (source + 1) * 40, :]
        for target, source in ((35, 37), (3, 1)):
            place = pl.ds(target, 22, stride=40)
            e1[place, :] = e1[place, :] + RATIO * e1[pl.ds(source, 22, stride=40), :]
        for place in (1, 37):
            e1[pl.ds(place, 22, stride=40), :] = jnp.zeros((22, 128), F32)

        def time_level2(n):
            t2[rows(n * 176, 176), :] = times(e1[rows(n * 176, 176), :], m2)

        loop(5, time_level2, unroll=5)

        def t2_row(i):
            return t2[i * 40 : (i + 1) * 40, :]

        p_now, q_after = t2_row(0), None
        for k in range(-2, 8):
            if k == 7:
                q_after, p_after = t2_row(20), None
            else:
                m = 1 if k == -2 else 6 + 2 * k
                even, odd = t2_row(m), t2_row(m + 1)
                q_after, p_after = q_of(even, odd), p_of(even, odd)
            n = (k + 2) * 40
            a2[0, n : n + 40, :] = low_of(p_now, q_after)
            a2[1, n : n + 40, :] = high_of(p_now, q_after)
            p_now = p_after
        a2[0, 400:440, :] = t2_row(3)
        a2[0, 440:480, :] = t2_row(21)

        def y_level2_of(xb, k):
            e = [a2[xb, pl.ds(k * 40 + j, 18, stride=2), :] for j in range(4)]
            return p_of(e[0], e[1]), q_of(e[2], e[3])

        def y_level2(k):
            place = rows(k * 24, 18)
            for xb in range(2):
                p, q = y_level2_of(xb, k)
                for yb in range(2):
                    value = high_of(p, q) if yb else low_of(p, q)
                    b = 2 * xb + yb
                    if b == 0:
                        e2[pl.ds(k * 24 + 2, 18), :] = value
                    c2[b, place, :] = shrink(old(c2, b, place, slice(None)) + value)

        def y_level2_low(k):
            e2[pl.ds(k * 24 + 2, 18), :] = low_of(*y_level2_of(0, k))

        for k in range(10, 12):
            y_level2_low(k)
        loop(10, y_level2, unroll=10)
        for source, target in ((38, 0), (39, 20)):
            e2[pl.ds(target, 12, stride=24), :] = a2[0, pl.ds(source, 12, stride=40), :]

        t3[...] = times(e2[...], m3)

        def t3_row(i):
            return t3[i * 24 : (i + 1) * 24, :]

        p_now = t3_row(10)
        for k in range(-2, 4):
            if k == 3:
                q_after, p_after = t3_row(11), None
            else:
                even, odd = t3_row(2 * k + 4), t3_row(2 * k + 5)
                q_after, p_after = q_of(even, odd), p_of(even, odd)
            n = (k + 2) * 24
            a3[0, n : n + 24, :] = low_of(p_now, q_after)
            a3[1, n : n + 24, :] = high_of(p_now, q_after)
            p_now = p_after

        lane = lax.broadcasted_iota(jnp.int32, (10, 128), 1)

        def y_level3(k):
            place = rows(k * 16, 10)
            for xb in range(2):
                e = [a3[xb, pl.ds(k * 24 + j, 10, stride=2), :] for j in range(4)]
                p, q = p_of(e[0], e[1]), q_of(e[2], e[3])
                for yb in range(2):
                    value = high_of(p, q) if yb else low_of(p, q)
                    b = 2 * xb + yb
                    value = old(c3, b, place, slice(None)) + value
                    if b == 0:
                        c3[b, place, :] = jnp.where(lane < 32, value, shrink(value))
                    else:
                        c3[b, place, :] = shrink(value)

        loop(6, y_level3, unroll=6)

        def up(low_now, high_now, low_before, high_before):
            p = low_now - RATIO * high_now
            q = high_before + RATIO * low_before
            return p + ROOT_THREE * q, ROOT_THREE * p - q

        for b in range(4):
            s3[b] = times(c3[b], m3t)

        def x_up3(k):
            for yb in range(2):
                e = [s3[b, rows((k + d) * 16, 16), :] for d in (1, 0) for b in (yb, 2 + yb)]
                even, odd = up(*e)
                p3[yb, rows(2 * k * 16, 16), :] = even
                p3[yb, rows((2 * k + 1) * 16, 16), :] = odd

        loop(5, x_up3, unroll=5)

        def y_up3(r):
            e = [p3[b, pl.ds(r * 16 + d, 9), :] for d in (1, 0) for b in (0, 1)]
            even, odd = up(*e)
            d2[pl.ds(r * 24, 9, stride=2), :] = even
            d2[pl.ds(r * 24 + 1, 9, stride=2), :] = odd

        loop(10, y_up3, unroll=10)

        lanes = lax.broadcasted_iota(jnp.int32, (240, 128), 1)
        for b in range(1, 4):
            s2[b] = times(c2[b], m2t)
        s2[0] = times(jnp.where(lanes < 64, d2[...], c2[0]), m2t)

        def x_up2(k):
            for yb in range(2):
                e = [s2[b, rows((k + d) * 24, 24), :] for d in (1, 0) for b in (yb, 2 + yb)]
                even, odd = up(*e)
                p2[yb, rows(2 * k * 24, 24), :] = even
                p2[yb, rows((2 * k + 1) * 24, 24), :] = odd

        loop(9, x_up2, unroll=9)

        def y_up2(r):
            e = [p2[b, pl.ds(r * 24 + d, 17), :] for d in (1, 0) for b in (0, 1)]
            even, odd = up(*e)
            d1[pl.ds(r * 40 + 6, 17, stride=2), :] = even
            d1[pl.ds(r * 40 + 7, 17, stride=2), :] = odd

        loop(17, lambda r: y_up2(r + 1), unroll=17)

        for piece in inner_rows:
            time_up1(0, [piece])

        up_parts = [(chunk, th) for chunk in range(4) for th in range(2)]

        def y_up1(row, chunk, th):
            result = []
            for xb in range(2):
                e = [
                    s1[th, 2 * xb + yb, pl.ds(row * 40 + d + 8 * chunk, 8), :]
                    for d in (8, 7) for yb in range(2)
                ]
                result.append(up(*e))
            return [(result[0][n], result[1][n]) for n in range(2)]

        def q_next(low, high):
            return high + RATIO * low

        def up1(first_k, i, qs):
            k = first_k + i
            after = []
            n = 0
            for chunk, th in up_parts:
                for parity, (low, high) in enumerate(y_up1(k + 1, chunk, th)):
                    p = low - RATIO * high
                    start = k * 128 + 16 * chunk + parity
                    reb[th, pl.ds(start, 8, stride=2), :] = p + ROOT_THREE * qs[n]
                    reb[th, pl.ds(start + 64, 8, stride=2), :] = ROOT_THREE * p - qs[n]
                    after.append(q_next(low, high))
                    n += 1
            return tuple(after)

        def q_start(row):
            return tuple(q_next(*one) for chunk, th in up_parts for one in y_up1(row, chunk, th))

        lax.fori_loop(0, 14, functools.partial(up1, 1), q_start(1), unroll=2)
        if not first:
            loop(28, lambda n: finish(n + 2))

        def ends():
            wait(f0)
            for tb in range(2):
                corners = [fcr[number, n, used + tb : used + tb + 1, :] for n, (_, used) in enumerate(CORNERS)]
                starts = []
                for ref, low_row, corner in ((qr, 72, corners[0]), (pr, 176, corners[2])):
                    after = ROOT_THREE * corner
                    low, place, high = (ref, 31, 63) if tb else (xr, low_row + 31, 95)
                    low[place : place + 1, :] = low[place : place + 1, :] + RATIO * after
                    ref[high : high + 1, :] = ref[high : high + 1, :] + after
                    starts.append(ref[96:97, :] if tb else xr[low_row - 70 : low_row - 69, :])
                for place, p, q, scale in (
                    (pl.ds(0, 1), corners[3], starts[1], 1.0),
                    (pl.ds(34, 1), corners[1], starts[0], 1.0 / ROOT_THREE),
                ):
                    cb[tb, place, :] = scale * low_of(p, q)
                    cb[2 + tb, place, :] = scale * high_of(p, q)
            level1_ends(inner, inner_last)
            level1_ends(edge, edge_last)
            column_before(lambda j: pl.ds(j, 2, stride=32), pl.ds(7, 2, stride=640))
            for b in range(4):
                time_up1(b, end_rows)
            up1(0, 0, q_start(0))
            up1(15, 0, q_start(15))

        return ends

    def finish(r):
        for th in range(2):
            out[r, :, th * 128 : (th + 1) * 128] = reb[th, rows(r * 64, 64), :]

    iteration(0)()
    iteration(1)()
    for r in (0, 1, 30, 31):
        finish(r)


def solution(mesh):
    nx, ny = mesh.shape["gx"], mesh.shape["gy"]

    def v(*shape):
        return pltpu.VMEM(shape, F32)

    def b(*shape):
        return pltpu.VMEM(shape, BF16)

    scratch = [
        pltpu.VMEM((32, 64, 256), jnp.int32), v(2048, 256), v(2048, 256),
        b(768, 256), b(768, 256), b(384, 128), b(384, 128), b(384, 128), b(384, 128),
        v(2, 32 * 72, 128), v(7, 17 * 40, 128), v(24 * 40, 128),
        v(22 * 40, 128), v(2, 12 * 40, 128), v(4, 10 * 24, 128), v(12 * 24, 128),
        v(12 * 24, 128), v(2, 6 * 24, 128), v(4, 6 * 16, 128),
        v(4, 6 * 16, 128), v(2, 10 * 16, 128), v(10 * 24, 128),
        v(4, 10 * 24, 128), v(2, 18 * 24, 128), v(18 * 40, 128),
        v(2, 4, 17 * 40, 128), v(2, 32 * 64, 128), v(4, 40, 128),
        v(2, 72, 128), v(2, 72, 128), v(104, 128), v(104, 128), v(4, 40, 128), v(2, 104, 128), v(2, 104, 128), v(2, 4, 40, 128),
        v(240, 128), v(7, 24, 128), v(2, 240, 128), v(2, 7, 24, 128), v(4, 24, 128), v(2, 4, 24, 128),
        pltpu.SemaphoreType.DMA((1,)), pltpu.SemaphoreType.DMA((24,)), pltpu.SemaphoreType.DMA((24,)),
    ]

    def on_device(counts):
        return pl.pallas_call(
            functools.partial(kernel, nx, ny),
            out_shape=jax.ShapeDtypeStruct(counts.shape, F32),
            in_specs=[pl.BlockSpec(memory_space=pltpu.HBM)],
            out_specs=pl.BlockSpec(memory_space=pltpu.VMEM),
            scratch_shapes=scratch,
            compiler_params=pltpu.CompilerParams(
                collective_id=0, has_side_effects=True, vmem_limit_bytes=50 * 1024 * 1024
            ),
        )(counts)

    spec = P(("grp", "gx"), "gy", None)
    return jax.shard_map(on_device, mesh=mesh, in_specs=(spec,), out_specs=spec, check_vma=False)
```
